256 devices in a mesh: snap: 64 (over z_hi, y, x, core), row: 4 (over z_lo).
Axes of the slice: x: 4, y: 4, z: 8 (z_hi: 2, z_lo: 4; z = z_hi * 4 + z_lo), core: 2. Of those that a mesh axis runs over, the one named last changes fastest.
Arguments:
- delay_matrix: float32 [128, 32, 16384], P('snap', 'row'), may hold values from -6 to 6
- arrangement: int32 [128], replicated, may hold values from 0 to 127, each once
- rotations: float32 [2, 64, 256, 256], P(None, 'snap'), may hold values from -1 to 2
Outputs:
- rotated: float32 [128, 32, 16384], P(None, 'row', 'snap')
- pair_grams: float32 [2, 64, 256, 256], P(None, 'snap', 'row')
The draws below stay inside these ranges and needn't reach their ends.
Inputs may be any that keep to these rules, and one draw needn't show every extreme that they name: arrangement names every block once.
All inputs are finite; a program needn't handle non-finite values.
Results may differ from the reference program's by a relative error of at most 0.00007.
Values sent between devices are 32-bit elements; how exact they have to be, the bound alone decides.
A program may use at most 128 MiB of HBM per device.

```python
import math
import jax
import jax.numpy as jnp
from jax import lax

MODES = 128
DELAYS = 32
B = 128
ROUNDS = 2
PAIRS = 64
BLOCKS = 128
COLUMNS = 16384


def draw_rotations(key, part):
    key = jax.random.fold_in(key, 7)
    order = 2 * B
    shape = (ROUNDS, PAIRS, order, order)
    noise = jnp.clip(jax.random.normal(key, shape, jnp.float32), -4.0, 4.0) * 0.35
    return jnp.eye(order, dtype=jnp.float32) + noise / math.sqrt(order)


def level_of(rng, shape, cuts, least, high):
    gain = 1.0
    for position, shards_of in cuts:
        steps = jax.random.uniform(jax.random.fold_in(jax.random.fold_in(rng, 6), position), (shards_of,), jnp.float32, least / len(cuts), high / len(cuts))
        gain = gain * jnp.repeat(jnp.exp(steps), shape[position] // shards_of).reshape((-1,) + (1,) * (len(shape) - 1 - position))
    return gain


def normal_values(rng, shape, width, most, shards=(), held_as=jnp.bfloat16):
    result = jax.random.normal(rng, shape, jnp.float32) * width
    if len(shards) > 0:
        result = level_of(rng, shape, shards, -0.22, 0.18) * result
    return jnp.clip(result, min=-most, max=most).astype(held_as)


def setup_inputs(seed: int = 0) -> dict:
    key_of = jax.random.split(jax.random.key(seed), 4)
    return {
        "delay_matrix": normal_values(key_of[0], (MODES, DELAYS, COLUMNS), 1.0, 6.0, ((0, 64), (1, 4)), jnp.float32),
        "arrangement": jax.random.permutation(key_of[1], BLOCKS).astype(jnp.int32),
        "rotations": draw_rotations(jax.random.fold_in(key_of[3], 71), 0),
    }


highest = lax.Precision.HIGHEST


def product(left_part, right_part):
    return jnp.dot(left_part, right_part, precision=highest, preferred_element_type=jnp.float32)


def one_round(first_blocks, second_blocks, rotation_set):
    def pair_step(item):
        first_part, second_part, rotation = item
        matrix = jnp.concatenate([first_part, second_part], axis=1)
        gram_part = product(matrix.T, matrix) / float(MODES * DELAYS)
        pair_gram = product(product(rotation.T, gram_part), rotation)
        turned = product(matrix, rotation)
        return turned[:, :B], turned[:, B:], pair_gram
    return lax.map(pair_step, (first_blocks, second_blocks, rotation_set))


def reference(delay_matrix, arrangement, rotations):
    row_count = MODES * DELAYS
    blocks = delay_matrix.reshape(row_count, BLOCKS, B).transpose(1, 0, 2)
    first_blocks = jnp.take(blocks, arrangement[0::2], axis=0)
    second_blocks = jnp.take(blocks, arrangement[1::2], axis=0)
    first_one, second_one, grams_one = one_round(first_blocks, second_blocks, rotations[0])
    second_one = jnp.roll(second_one, 1, axis=0)
    first_two, second_two, grams_two = one_round(first_one, second_one, rotations[1])
    joined = jnp.stack([first_two, second_two], axis=1)
    rotated = joined.transpose(2, 0, 1, 3).reshape(MODES, DELAYS, COLUMNS)
    return rotated, jnp.stack([grams_one, grams_two])
```

```python
import functools

import jax
import jax.numpy as jnp
from jax import lax
from jax.experimental import pallas as pl
from jax.experimental.pallas import tpu as pltpu
from jax.sharding import PartitionSpec as P

MESH = pl.DeviceIdType.MESH
GROUPS = 8


def split(value):
    high = value.astype(jnp.bfloat16)
    low = (value - high.astype(jnp.float32)).astype(jnp.bfloat16)
    return high, low


def dot(left, right):
    return jnp.dot(left, right, preferred_element_type=jnp.float32)


def dot_rows(left, right):
    return lax.dot_general(left, right, (((0,), (0,)), ((), ())), preferred_element_type=jnp.float32)


def kernel(
    sizes,
    order_ref,
    x_ref,
    rot_ref,
    out_ref,
    gram_ref,
    stage,
    blocks,
    first,
    second,
    arrived,
    result,
    rot_high,
    rot_low,
    sums,
    shares,
    share_in,
    a2a_send,
    a2a_recv,
    next_send,
    next_recv,
    out_sem,
    share_send,
    share_recv,
):
    snaps, rows, modes, delays, width = sizes
    half = width // 2
    per_group = snaps // GROUPS
    group_modes = modes * per_group
    group_rows = group_modes * delays
    share_rows = width // rows
    scale = 1.0 / float(modes * snaps * delays * rows)

    me = lax.axis_index("snap")
    row = lax.axis_index("row")
    my_group = me // per_group
    after = (me + 1) % snaps

    barrier = pltpu.get_barrier_semaphore()

    @pl.loop(1, snaps)
    def _(i):
        pl.semaphore_signal(
            barrier, inc=1, device_id={"snap": (me + i) % snaps, "row": row}, device_id_type=MESH
        )

    for i in range(1, rows):
        pl.semaphore_signal(
            barrier, inc=1, device_id={"snap": me, "row": (row + i) % rows}, device_id_type=MESH
        )

    @pl.loop(0, snaps, unroll=4)
    def _(d):
        stage[d, :, :, :half] = x_ref[:, order_ref[2 * d]]
        stage[d, :, :, half:] = x_ref[:, order_ref[2 * d + 1]]

    for r in range(2):
        high, low = split(rot_ref[r, 0])
        rot_high[r] = high
        rot_low[r] = low
    sums[...] = jnp.zeros_like(sums)
    blocks[pl.ds(me * modes, modes)] = stage[me]

    pl.semaphore_wait(barrier, snaps - 1 + rows - 1)

    def send_blocks(d):
        pltpu.make_async_remote_copy(
            src_ref=stage.at[d],
            dst_ref=blocks.at[pl.ds(me * modes, modes)],
            send_sem=a2a_send,
            recv_sem=a2a_recv.at[my_group],
            device_id={"snap": d, "row": row},
            device_id_type=MESH,
        ).start()

    low_part = me % (snaps // 2)
    high_part = me // (snaps // 2)
    ys = GROUPS // 2
    my_y = my_group % ys
    my_place = me % per_group

    @pl.loop(0, ys)
    def _(k):
        @pl.loop(0, per_group)
        def _(j):
            place = ((my_y + k) % ys) * per_group + (my_place + j) % per_group
            send_blocks((1 - high_part) * (snaps // 2) + place)

            @pl.when(k + j > 0)
            def _():
                send_blocks(high_part * (snaps // 2) + place)

    def wait_group(group):
        whole = blocks.at[pl.ds(0, group_modes)]
        part = blocks.at[pl.ds(0, group_modes - modes)]

        @pl.when(group == my_group)
        def _():
            pltpu.make_async_copy(part, part, a2a_recv.at[group]).wait()

        @pl.when(group != my_group)
        def _():
            pltpu.make_async_copy(whole, whole, a2a_recv.at[group]).wait()

    def turn(r, matrix):
        high, low = split(matrix)
        turned = dot(high, rot_high[r]) + (dot(high, rot_low[r]) + dot(low, rot_high[r]))
        high, low = split(turned)
        sums[r, :, :width] += dot_rows(high, high)
        sums[r, :, width:] += dot_rows(high, low)
        return turned

    def send_next(group):
        span = pl.ds(group * group_modes, group_modes)
        return pltpu.make_async_remote_copy(
            src_ref=second.at[span],
            dst_ref=arrived.at[span],
            send_sem=next_send,
            recv_sem=next_recv.at[group],
            device_id={"snap": after, "row": row},
            device_id_type=MESH,
        )

    def group_at(k, turned_by):
        part = (high_part + k // ys) % 2
        return part * ys + (my_y + ys - (k + turned_by) % ys) % ys

    def round_one(k):
        group = group_at(k, 0)
        span = pl.ds(group * group_modes, group_modes)
        wait_group(group)
        turned = turn(0, blocks[span].reshape(group_rows, width))
        turned = turned.reshape(group_modes, delays, width)
        first[span] = turned[:, :, :half]
        second[span] = turned[:, :, half:]
        send_next(group).start()

    wraps = jnp.where(my_place == 0, 1, 0)

    def round_two(k):
        group = group_at(k, wraps)
        span = pl.ds(group * group_modes, group_modes)
        send_next(group).wait_recv()
        matrix = jnp.concatenate([first[span], arrived[span]], axis=2)
        turned = turn(1, matrix.reshape(group_rows, width))
        result[span] = turned.reshape(group_modes, delays, width)
        pltpu.make_async_copy(result.at[span], out_ref.at[span], out_sem).start()

    def finish(r):
        cross = sums[r, :, width:]
        total = (sums[r, :, :width] + (cross + cross.T)) * scale
        shares[r] = total.reshape(rows, share_rows, width)
        for i in range(1, rows):
            share_copy(r, i).start()

    def share_copy(r, i):
        to = (row + i) % rows
        return pltpu.make_async_remote_copy(
            src_ref=shares.at[r, to],
            dst_ref=share_in.at[r, i],
            send_sem=share_send.at[r, i],
            recv_sem=share_recv.at[r, i],
            device_id={"snap": me, "row": to},
            device_id_type=MESH,
        )

    def collect(r):
        for i in range(1, rows):
            share_copy(r, i).wait()
        total = shares[r, row]
        for i in range(1, rows):
            total = total + share_in[r, i]
        gram_ref[r, 0] = total

    round_one(0)

    @pl.loop(1, GROUPS)
    def _(k):
        round_one(k)
        round_two(k - 1)

    finish(0)
    round_two(GROUPS - 1)
    finish(1)
    collect(0)
    everything = stage.at[pl.ds(0, snaps - 1)]
    pltpu.make_async_copy(everything, everything, a2a_send).wait()
    pltpu.make_async_copy(second, second, next_send).wait()
    pltpu.make_async_copy(result, out_ref, out_sem).wait()
    collect(1)


def body(delay_matrix, arrangement, rotations):
    modes, delays, columns = delay_matrix.shape
    snaps = lax.axis_size("snap")
    rows = lax.axis_size("row")
    width = columns // snaps
    half = width // 2
    share_rows = width // rows
    sizes = (snaps, rows, modes, delays, width)
    f32, bf16 = jnp.float32, jnp.bfloat16
    blocks = delay_matrix.reshape(modes, delays, 2 * snaps, half).transpose(0, 2, 1, 3)
    vmem = pl.BlockSpec(memory_space=pltpu.VMEM)
    return pl.pallas_call(
        functools.partial(kernel, sizes),
        out_shape=(
            jax.ShapeDtypeStruct((snaps * modes, delays, width), f32),
            jax.ShapeDtypeStruct((2, 1, share_rows, width), f32),
        ),
        in_specs=[pl.BlockSpec(memory_space=pltpu.SMEM), vmem, vmem],
        out_specs=(pl.BlockSpec(memory_space=pl.ANY), vmem),
        scratch_shapes=[
            pltpu.VMEM((snaps, modes, delays, width), f32),
            pltpu.VMEM((snaps * modes, delays, width), f32),
            pltpu.VMEM((snaps * modes, delays, half), f32),
            pltpu.VMEM((snaps * modes, delays, half), f32),
            pltpu.VMEM((snaps * modes, delays, half), f32),
            pltpu.VMEM((snaps * modes, delays, width), f32),
            pltpu.VMEM((2, width, width), bf16),
            pltpu.VMEM((2, width, width), bf16),
            pltpu.VMEM((2, width, 2 * width), f32),
            pltpu.VMEM((2, rows, share_rows, width), f32),
            pltpu.VMEM((2, rows, share_rows, width), f32),
            pltpu.SemaphoreType.DMA,
            pltpu.SemaphoreType.DMA((GROUPS,)),
            pltpu.SemaphoreType.DMA,
            pltpu.SemaphoreType.DMA((GROUPS,)),
            pltpu.SemaphoreType.DMA,
            pltpu.SemaphoreType.DMA((2, rows)),
            pltpu.SemaphoreType.DMA((2, rows)),
        ],
        compiler_params=pltpu.CompilerParams(
            collective_id=0, has_side_effects=True, vmem_limit_bytes=32 * 1024 * 1024
        ),
        name="rounds",
    )(arrangement, blocks, rotations)


def solution(mesh):
    placed = (P("snap", "row", None), P(), P(None, "snap", None, None))
    return jax.shard_map(
        body,
        mesh=mesh,
        in_specs=placed,
        out_specs=(P(None, "row", "snap"), P(None, "snap", "row", None)),
        check_vma=False,
    )
```

```python
import functools

import jax
import jax.numpy as jnp
from jax import lax
from jax.experimental import pallas as pl
from jax.experimental.pallas import tpu as pltpu
from jax.sharding import PartitionSpec as P

MESH = pl.DeviceIdType.MESH
GROUPS = 8


def split(value):
    high = value.astype(jnp.bfloat16)
    low = (value - high.astype(jnp.float32)).astype(jnp.bfloat16)
    return high, low


def dot(left, right):
    return jnp.dot(left, right, preferred_element_type=jnp.float32)


def dot_rows(left, right):
    return lax.dot_general(left, right, (((0,), (0,)), ((), ())), preferred_element_type=jnp.float32)


def kernel(
    sizes,
    order_hbm,
    x_hbm,
    rot_hbm,
    out_ref,
    gram_ref,
    order_ref,
    x_ref,
    rot_ref,
    rot_before,
    stage,
    blocks,
    extra,
    first,
    second,
    arrived,
    result,
    rot_high,
    rot_low,
    before_high,
    before_low,
    sums,
    shares,
    share_in,
    load_sem,
    a2a_send,
    a2a_recv,
    extra_send,
    extra_recv,
    before_send,
    before_recv,
    next_send,
    next_recv,
    out_sem,
    share_send,
    share_recv,
):
    snaps, rows, modes, delays, width = sizes
    half = width // 2
    per_group = snaps // GROUPS
    group_modes = modes * per_group
    group_rows = group_modes * delays
    share_rows = width // rows
    scale = 1.0 / float(modes * snaps * delays * rows)

    me = lax.axis_index("snap")
    row = lax.axis_index("row")
    my_group = me // per_group
    after = (me + 1) % snaps
    run = snaps // 2
    is_head = me % run == 0
    is_last = me % run == run - 1

    loads = [
        pltpu.make_async_copy(order_hbm, order_ref, load_sem.at[0]),
        pltpu.make_async_copy(x_hbm, x_ref, load_sem.at[1]),
        pltpu.make_async_copy(rot_hbm, rot_ref, load_sem.at[2]),
    ]
    for load in loads:
        load.start()

    barrier = pltpu.get_barrier_semaphore()

    @pl.loop(1, snaps)
    def _(i):
        pl.semaphore_signal(
            barrier, inc=1, device_id={"snap": (me + i) % snaps, "row": row}, device_id_type=MESH
        )

    for i in range(1, rows):
        pl.semaphore_signal(
            barrier, inc=1, device_id={"snap": me, "row": (row + i) % rows}, device_id_type=MESH
        )

    for load in loads:
        load.wait()

    @pl.loop(0, snaps, unroll=4)
    def _(d):
        stage[d, :, :, :half] = x_ref[:, order_ref[2 * d]]
        stage[d, :, :, half:] = x_ref[:, order_ref[2 * d + 1]]

    for r in range(2):
        high, low = split(rot_ref[r, 0])
        rot_high[r] = high
        rot_low[r] = low
    sums[...] = jnp.zeros_like(sums)
    blocks[pl.ds(me * modes, modes)] = stage[me]

    @pl.when(is_head)
    def _():
        extra[pl.ds(me * modes, modes)] = stage[(me + snaps - 1) % snaps]

    pl.semaphore_wait(barrier, snaps - 1 + rows - 1)

    before_copy = pltpu.make_async_remote_copy(
        src_ref=rot_ref.at[0, 0, :, pl.ds(half, half)],
        dst_ref=rot_before,
        send_sem=before_send,
        recv_sem=before_recv,
        device_id={"snap": after, "row": row},
        device_id_type=MESH,
    )

    @pl.when(is_last)
    def _():
        before_copy.start()

    def send_blocks(d):
        pltpu.make_async_remote_copy(
            src_ref=stage.at[d],
            dst_ref=blocks.at[pl.ds(me * modes, modes)],
            send_sem=a2a_send,
            recv_sem=a2a_recv.at[my_group],
            device_id={"snap": d, "row": row},
            device_id_type=MESH,
        ).start()

        @pl.when(d % run == 0)
        def _():
            pltpu.make_async_remote_copy(
                src_ref=stage.at[(d + snaps - 1) % snaps],
                dst_ref=extra.at[pl.ds(me * modes, modes)],
                send_sem=extra_send,
                recv_sem=extra_recv.at[my_group],
                device_id={"snap": d, "row": row},
                device_id_type=MESH,
            ).start()

    high_part = me // run
    ys = GROUPS // 2
    my_y = my_group % ys
    my_place = me % per_group

    @pl.loop(0, ys)
    def _(k):
        @pl.loop(0, per_group)
        def _(j):
            place = ((my_y + k) % ys) * per_group + (my_place + j) % per_group
            send_blocks((1 - high_part) * run + place)

            @pl.when(k + j > 0)
            def _():
                send_blocks(high_part * run + place)

    def wait_group(buffer, sems, group):
        whole = buffer.at[pl.ds(0, group_modes)]
        part = buffer.at[pl.ds(0, group_modes - modes)]

        @pl.when(group == my_group)
        def _():
            pltpu.make_async_copy(part, part, sems.at[group]).wait()

        @pl.when(group != my_group)
        def _():
            pltpu.make_async_copy(whole, whole, sems.at[group]).wait()

    @pl.when(is_head)
    def _():
        before_copy.wait_recv()
        high, low = split(rot_before[...])
        before_high[...] = high
        before_low[...] = low

    def turn(r, matrix):
        high, low = split(matrix)
        turned = dot(high, rot_high[r]) + (dot(high, rot_low[r]) + dot(low, rot_high[r]))
        high, low = split(turned)
        sums[r, :, :width] += dot_rows(high, high)
        sums[r, :, width:] += dot_rows(high, low)
        return turned

    def send_next(group):
        span = pl.ds(group * group_modes, group_modes)
        return pltpu.make_async_remote_copy(
            src_ref=second.at[span],
            dst_ref=arrived.at[span],
            send_sem=next_send,
            recv_sem=next_recv.at[group],
            device_id={"snap": after, "row": row},
            device_id_type=MESH,
        )

    def group_at(k, turned_by):
        part = (high_part + k // ys) % 2
        return part * ys + (my_y + ys - (k + turned_by) % ys) % ys

    def round_one(k):
        group = group_at(k, 0)
        span = pl.ds(group * group_modes, group_modes)
        wait_group(blocks, a2a_recv, group)
        turned = turn(0, blocks[span].reshape(group_rows, width))
        turned = turned.reshape(group_modes, delays, width)
        first[span] = turned[:, :, :half]
        second[span] = turned[:, :, half:]

        @pl.when(jnp.logical_not(is_last))
        def _():
            send_next(group).start()

        @pl.when(is_head)
        def _():
            wait_group(extra, extra_recv, group)
            high, low = split(extra[span].reshape(group_rows, width))
            turned = dot(high, before_high[...]) + (
                dot(high, before_low[...]) + dot(low, before_high[...])
            )
            arrived[span] = turned.reshape(group_modes, delays, half)

    wraps = jnp.where(jnp.logical_and(my_place == 0, jnp.logical_not(is_head)), 1, 0)

    def round_two(k):
        group = group_at(k, wraps)
        span = pl.ds(group * group_modes, group_modes)

        @pl.when(jnp.logical_not(is_head))
        def _():
            send_next(group).wait_recv()

        matrix = jnp.concatenate([first[span], arrived[span]], axis=2)
        turned = turn(1, matrix.reshape(group_rows, width))
        result[span] = turned.reshape(group_modes, delays, width)
        pltpu.make_async_copy(result.at[span], out_ref.at[span], out_sem).start()

    def finish(r):
        cross = sums[r, :, width:]
        total = (sums[r, :, :width] + (cross + cross.T)) * scale
        shares[r] = total.reshape(rows, share_rows, width)
        for i in range(1, rows):
            share_copy(r, i).start()

    def share_copy(r, i):
        to = (row + i) % rows
        return pltpu.make_async_remote_copy(
            src_ref=shares.at[r, to],
            dst_ref=share_in.at[r, i],
            send_sem=share_send.at[r, i],
            recv_sem=share_recv.at[r, i],
            device_id={"snap": me, "row": to},
            device_id_type=MESH,
        )

    def collect(r):
        for i in range(1, rows):
            share_copy(r, i).wait()
        total = shares[r, row]
        for i in range(1, rows):
            total = total + share_in[r, i]
        gram_ref[r, 0] = total

    round_one(0)

    @pl.loop(1, GROUPS)
    def _(k):
        round_one(k)
        round_two(k - 1)

    finish(0)
    round_two(GROUPS - 1)
    finish(1)
    collect(0)
    everything = stage.at[pl.ds(0, snaps - 1)]
    pltpu.make_async_copy(everything, everything, a2a_send).wait()
    two = stage.at[pl.ds(0, 2)]
    one = stage.at[0]

    @pl.when(is_head)
    def _():
        pltpu.make_async_copy(one, one, extra_send).wait()

    @pl.when(jnp.logical_not(is_head))
    def _():
        pltpu.make_async_copy(two, two, extra_send).wait()

    @pl.when(is_last)
    def _():
        before_copy.wait_send()

    @pl.when(jnp.logical_not(is_last))
    def _():
        pltpu.make_async_copy(second, second, next_send).wait()

    pltpu.make_async_copy(result, out_ref, out_sem).wait()
    collect(1)


def body(delay_matrix, arrangement, rotations):
    modes, delays, columns = delay_matrix.shape
    snaps = lax.axis_size("snap")
    rows = lax.axis_size("row")
    width = columns // snaps
    half = width // 2
    share_rows = width // rows
    sizes = (snaps, rows, modes, delays, width)
    f32, bf16 = jnp.float32, jnp.bfloat16
    blocks = delay_matrix.reshape(modes, delays, 2 * snaps, half).transpose(0, 2, 1, 3)
    vmem = pl.BlockSpec(memory_space=pltpu.VMEM)
    hbm = pl.BlockSpec(memory_space=pltpu.HBM)
    return pl.pallas_call(
        functools.partial(kernel, sizes),
        out_shape=(
            jax.ShapeDtypeStruct((snaps * modes, delays, width), f32),
            jax.ShapeDtypeStruct((2, 1, share_rows, width), f32),
        ),
        in_specs=[hbm, hbm, hbm],
        out_specs=(hbm, vmem),
        scratch_shapes=[
            pltpu.SMEM(arrangement.shape, arrangement.dtype),
            pltpu.VMEM(blocks.shape, f32),
            pltpu.VMEM(rotations.shape, f32),
            pltpu.VMEM((width, half), f32),
            pltpu.VMEM((snaps, modes, delays, width), f32),
            pltpu.VMEM((snaps * modes, delays, width), f32),
            pltpu.VMEM((snaps * modes, delays, width), f32),
            pltpu.VMEM((snaps * modes, delays, half), f32),
            pltpu.VMEM((snaps * modes, delays, half), f32),
            pltpu.VMEM((snaps * modes, delays, half), f32),
            pltpu.VMEM((snaps * modes, delays, width), f32),
            pltpu.VMEM((2, width, width), bf16),
            pltpu.VMEM((2, width, width), bf16),
            pltpu.VMEM((width, half), bf16),
            pltpu.VMEM((width, half), bf16),
            pltpu.VMEM((2, width, 2 * width), f32),
            pltpu.VMEM((2, rows, share_rows, width), f32),
            pltpu.VMEM((2, rows, share_rows, width), f32),
            pltpu.SemaphoreType.DMA((3,)),
            pltpu.SemaphoreType.DMA,
            pltpu.SemaphoreType.DMA((GROUPS,)),
            pltpu.SemaphoreType.DMA,
            pltpu.SemaphoreType.DMA((GROUPS,)),
            pltpu.SemaphoreType.DMA,
            pltpu.SemaphoreType.DMA,
            pltpu.SemaphoreType.DMA,
            pltpu.SemaphoreType.DMA((GROUPS,)),
            pltpu.SemaphoreType.DMA,
            pltpu.SemaphoreType.DMA((2, rows)),
            pltpu.SemaphoreType.DMA((2, rows)),
        ],
        compiler_params=pltpu.CompilerParams(
            collective_id=0, has_side_effects=True, vmem_limit_bytes=60 * 1024 * 1024
        ),
        name="rounds",
    )(arrangement, blocks, rotations)


def solution(mesh):
    placed = (P("snap", "row", None), P(), P(None, "snap", None, None))
    return jax.shard_map(
        body,
        mesh=mesh,
        in_specs=placed,
        out_specs=(P(None, "row", "snap"), P(None, "snap", "row", None)),
        check_vma=False,
    )
```

```python
import functools

import jax
import jax.numpy as jnp
from jax import lax
from jax.experimental import pallas as pl
from jax.experimental.pallas import tpu as pltpu
from jax.sharding import PartitionSpec as P

MESH = pl.DeviceIdType.MESH
RELAY_LAG = 2
GROUPS = 8


def split(value):
    high = value.astype(jnp.bfloat16)
    low = (value - high.astype(jnp.float32)).astype(jnp.bfloat16)
    return high, low


def dot(left, right):
    return jnp.dot(left, right, preferred_element_type=jnp.float32)


def dot_rows(left, right):
    return lax.dot_general(left, right, (((0,), (0,)), ((), ())), preferred_element_type=jnp.float32)


def kernel(
    sizes,
    order_hbm,
    x_hbm,
    rot_hbm,
    out_ref,
    gram_out,
    order_ref,
    x_ref,
    rot_ref,
    rot_before,
    stage,
    extra_stage,
    blocks,
    extra,
    first,
    second,
    arrived,
    relayed,
    result,
    rot_high,
    rot_low,
    before_high,
    before_low,
    sums,
    shares,
    share_in,
    gram_ref,
    load_sem,
    a2a_send,
    a2a_recv,
    extra_send,
    extra_recv,
    before_send,
    before_recv,
    next_send,
    next_recv,
    relay_send,
    relay_recv,
    out_sem,
    gram_sem,
    share_send,
    share_recv,
):
    snaps, rows, modes, delays, width = sizes
    half = width // 2
    per_group = snaps // GROUPS
    group_modes = modes * per_group
    group_rows = group_modes * delays
    share_rows = width // rows
    scale = 1.0 / float(modes * snaps * delays * rows)

    me = lax.axis_index("snap")
    row = lax.axis_index("row")
    my_group = me // per_group
    after = (me + 1) % snaps
    run = snaps // 2
    high_part = me // run
    is_head = me % run == 0
    is_last = me % run == run - 1
    in_low, in_high = high_part == 0, high_part == 1
    hands_over = jnp.logical_and(is_last, in_high)

    loads = [
        pltpu.make_async_copy(order_hbm, order_ref, load_sem.at[0]),
        pltpu.make_async_copy(x_hbm, x_ref, load_sem.at[1]),
        pltpu.make_async_copy(rot_hbm, rot_ref, load_sem.at[2]),
    ]
    for load in loads:
        load.start()

    barrier = pltpu.get_barrier_semaphore()

    @pl.loop(1, snaps)
    def _(i):
        pl.semaphore_signal(
            barrier, inc=1, device_id={"snap": (me + i) % snaps, "row": row}, device_id_type=MESH
        )

    for i in range(1, rows):
        pl.semaphore_signal(
            barrier, inc=1, device_id={"snap": me, "row": (row + i) % rows}, device_id_type=MESH
        )

    for load in loads:
        load.wait()

    pl.semaphore_wait(barrier, snaps - 1 + rows - 1)

    before_copy = pltpu.make_async_remote_copy(
        src_ref=rot_ref.at[0, 0, :, pl.ds(half, half)],
        dst_ref=rot_before,
        send_sem=before_send,
        recv_sem=before_recv,
        device_id={"snap": after, "row": row},
        device_id_type=MESH,
    )

    @pl.when(is_last)
    def _():
        before_copy.start()

    def send_blocks(d):
        stage[d, :, :, :half] = x_ref[:, order_ref[2 * d]]
        stage[d, :, :, half:] = x_ref[:, order_ref[2 * d + 1]]
        pltpu.make_async_remote_copy(
            src_ref=stage.at[d],
            dst_ref=blocks.at[pl.ds(me * modes, modes)],
            send_sem=a2a_send,
            recv_sem=a2a_recv.at[my_group],
            device_id={"snap": d, "row": row},
            device_id_type=MESH,
        ).start()

        @pl.when(jnp.logical_or(d == run, d == high_part * run))
        def _():
            send_extra(d)

    def send_extra(head):
        before = (head + snaps - 1) % snaps
        place = head // run
        extra_stage[place, :, :, :half] = x_ref[:, order_ref[2 * before]]
        extra_stage[place, :, :, half:] = x_ref[:, order_ref[2 * before + 1]]
        pltpu.make_async_remote_copy(
            src_ref=extra_stage.at[place],
            dst_ref=extra.at[pl.ds(me * modes, modes)],
            send_sem=extra_send,
            recv_sem=extra_recv.at[my_group],
            device_id={"snap": head, "row": row},
            device_id_type=MESH,
        ).start()

    ys = GROUPS // 2
    my_y = my_group % ys
    my_place = me % per_group

    def place_at(i):
        k, j = i // per_group, i % per_group
        return ((my_y + k) % ys) * per_group + (my_place + j) % per_group

    @pl.loop(0, run)
    def _(i):
        send_blocks((1 - high_part) * run + place_at(i))

        @pl.when(2 * i < run)
        def _():
            @pl.when(i > 0)
            def _():
                send_blocks(high_part * run + place_at(2 * i))

            send_blocks(high_part * run + place_at(2 * i + 1))

    stage[me, :, :, :half] = x_ref[:, order_ref[2 * me]]
    stage[me, :, :, half:] = x_ref[:, order_ref[2 * me + 1]]
    blocks[pl.ds(me * modes, modes)] = stage[me]


    @pl.when(is_head)
    def _():
        before = (me + snaps - 1) % snaps
        extra[pl.ds(me * modes, modes), :, :half] = x_ref[:, order_ref[2 * before]]
        extra[pl.ds(me * modes, modes), :, half:] = x_ref[:, order_ref[2 * before + 1]]

    for r in range(2):
        high, low = split(rot_ref[r, 0])
        rot_high[r] = high
        rot_low[r] = low
    sums[...] = jnp.zeros_like(sums)

    def wait_group(buffer, sems, group):
        whole = buffer.at[pl.ds(0, group_modes)]
        part = buffer.at[pl.ds(0, group_modes - modes)]

        @pl.when(group == my_group)
        def _():
            pltpu.make_async_copy(part, part, sems.at[group]).wait()

        @pl.when(group != my_group)
        def _():
            pltpu.make_async_copy(whole, whole, sems.at[group]).wait()

    def turn(r, matrix):
        high, low = split(matrix)
        return dot(high, rot_high[r]) + (dot(high, rot_low[r]) + dot(low, rot_high[r]))

    def add_gram(r, turned):
        high, low = split(turned)
        sums[r, :, :width] += dot_rows(high, high)
        sums[r, :, width:] += dot_rows(high, low)

    def send_next(group):
        span = pl.ds(group * group_modes, group_modes)
        return pltpu.make_async_remote_copy(
            src_ref=second.at[span],
            dst_ref=arrived.at[span],
            send_sem=next_send,
            recv_sem=next_recv.at[group],
            device_id={"snap": after, "row": row},
            device_id_type=MESH,
        )

    def to_relay(group, step):
        return pltpu.make_async_remote_copy(
            src_ref=second.at[pl.ds(group * group_modes, group_modes)],
            dst_ref=relayed,
            send_sem=next_send,
            recv_sem=relay_recv,
            device_id={"snap": me - step * per_group, "row": row},
            device_id_type=MESH,
        )

    relay_step = ys - 1 - my_y
    is_relay = jnp.logical_and(my_place == per_group - 1, jnp.logical_and(in_high, relay_step > 0))
    relay_group = high_part * ys + ys - 1 - relay_step
    relay_out = pltpu.make_async_remote_copy(
        src_ref=relayed,
        dst_ref=arrived.at[pl.ds(relay_group * group_modes, group_modes)],
        send_sem=relay_send,
        recv_sem=next_recv.at[relay_group],
        device_id={"snap": (high_part * run + run) % snaps, "row": row},
        device_id_type=MESH,
    )

    def pass_on(k):
        @pl.when(jnp.logical_and(is_relay, k == relay_step + RELAY_LAG))
        def _():
            pltpu.make_async_copy(relayed, relayed, relay_recv).wait()
            relay_out.start()

    def group_of(crossing, k):
        return (high_part + crossing) % 2 * ys + (my_y + ys - k % ys) % ys

    def in_order(i):
        crossing = jnp.where(jnp.logical_or(i == 2, i >= 5), 1, 0)
        before = jnp.where(i >= 5, i - 4, jnp.where(i == 2, 0, jnp.where(i > 2, i - 1, i)))
        return crossing, before

    def round_one(k):
        group = group_of(*in_order(k))
        span = pl.ds(group * group_modes, group_modes)
        wait_group(blocks, a2a_recv, group)
        turned = turn(0, blocks[span].reshape(group_rows, width))
        first[span] = turned[:, :half].reshape(group_modes, delays, half)
        second[span] = turned[:, half:].reshape(group_modes, delays, half)
        crossing, step = in_order(k)

        @pl.when(jnp.logical_or(jnp.logical_not(is_last), jnp.logical_and(hands_over, crossing + step == 0)))
        def _():
            send_next(group).start()

        @pl.when(jnp.logical_and(hands_over, jnp.logical_and(crossing == 0, step > 0)))
        def _():
            to_relay(group, step).start()

        add_gram(0, turned)

    wraps = jnp.logical_and(my_place == 0, me != run)

    def round_two(k):
        @pl.when(jnp.logical_and(is_head, k == 0))
        def _():
            before_copy.wait_recv()
            high, low = split(rot_before[...])
            before_high[...] = high
            before_low[...] = low

        crossing, step = in_order(k)
        group = jnp.where(wraps, group_of(k // ys, k % ys + 1), group_of(crossing, step))
        span = pl.ds(group * group_modes, group_modes)

        raw = jnp.logical_and(is_head, jnp.logical_or(in_high, group // ys == 0))

        @pl.when(jnp.logical_not(raw))
        def _():
            send_next(group).wait_recv()

        @pl.when(raw)
        def _():
            wait_group(extra, extra_recv, group)
            high, low = split(extra[span].reshape(group_rows, width))
            turned = dot(high, before_high[...]) + (
                dot(high, before_low[...]) + dot(low, before_high[...])
            )
            arrived[span] = turned.reshape(group_modes, delays, half)

        matrix = jnp.concatenate([first[span], arrived[span]], axis=2)
        turned = turn(1, matrix.reshape(group_rows, width))
        result[span] = turned.reshape(group_modes, delays, width)
        pltpu.make_async_copy(result.at[span], out_ref.at[span], out_sem).start()
        add_gram(1, turned)

    def finish(r):
        cross = sums[r, :, width:]
        total = (sums[r, :, :width] + (cross + cross.T)) * scale
        shares[r] = total.reshape(rows, share_rows, width)
        for i in range(1, rows):
            share_copy(r, i).start()

    def share_copy(r, i):
        to = (row + i) % rows
        return pltpu.make_async_remote_copy(
            src_ref=shares.at[r, to],
            dst_ref=share_in.at[r, i],
            send_sem=share_send.at[r, i],
            recv_sem=share_recv.at[r, i],
            device_id={"snap": me, "row": to},
            device_id_type=MESH,
        )

    def collect(r):
        for i in range(1, rows):
            share_copy(r, i).wait()
        total = shares[r, row]
        for i in range(1, rows):
            total = total + share_in[r, i]
        gram_ref[r, 0] = total
        pltpu.make_async_copy(gram_ref.at[r], gram_out.at[r], gram_sem.at[r]).start()

    round_one(0)
    round_one(1)

    @pl.loop(2, GROUPS)
    def _(k):
        pass_on(k)
        round_one(k)
        round_two(k - 2)

    finish(0)
    round_two(GROUPS - 2)
    round_two(GROUPS - 1)
    finish(1)
    collect(0)
    everything = stage.at[pl.ds(0, snaps - 1)]
    pltpu.make_async_copy(everything, everything, a2a_send).wait()
    one = extra_stage.at[0]

    @pl.when(jnp.logical_and(in_low, me > 0))
    def _():
        pltpu.make_async_copy(extra_stage, extra_stage, extra_send).wait()

    @pl.when(jnp.logical_or(me == 0, me > run))
    def _():
        pltpu.make_async_copy(one, one, extra_send).wait()

    @pl.when(is_relay)
    def _():
        relay_out.wait_send()

    @pl.when(is_last)
    def _():
        before_copy.wait_send()

    @pl.when(hands_over)
    def _():
        sent = second.at[pl.ds(0, run * modes)]
        pltpu.make_async_copy(sent, sent, next_send).wait()

    @pl.when(jnp.logical_not(is_last))
    def _():
        pltpu.make_async_copy(second, second, next_send).wait()

    pltpu.make_async_copy(result, out_ref, out_sem).wait()
    collect(1)
    for r in range(2):
        pltpu.make_async_copy(gram_ref.at[r], gram_out.at[r], gram_sem.at[r]).wait()


def write_results(out_from, gram_from, out_ref, gram_ref, out_held, gram_held, in_sem, out_sem):
    pieces = in_sem.shape[0] - 1
    length = out_ref.shape[0] // pieces
    spans = [pl.ds(i * length, length) for i in range(pieces)]
    steps = [(out_from.at[span], out_held.at[span], out_ref.at[span]) for span in spans]
    steps.append((gram_from, gram_held, gram_ref))
    loads = [pltpu.make_async_copy(a, b, in_sem.at[i]) for i, (a, b, _) in enumerate(steps)]
    stores = [pltpu.make_async_copy(b, c, out_sem.at[i]) for i, (_, b, c) in enumerate(steps)]
    for load in loads:
        load.start()
    for load, store in zip(loads, stores):
        load.wait()
        store.start()
    for store in stores:
        store.wait()


def body(delay_matrix, arrangement, rotations):
    modes, delays, columns = delay_matrix.shape
    snaps = lax.axis_size("snap")
    rows = lax.axis_size("row")
    width = columns // snaps
    half = width // 2
    share_rows = width // rows
    sizes = (snaps, rows, modes, delays, width)
    f32, bf16 = jnp.float32, jnp.bfloat16
    blocks = delay_matrix.reshape(modes, delays, 2 * snaps, half).transpose(0, 2, 1, 3)
    hbm = pl.BlockSpec(memory_space=pltpu.HBM)
    out_shape = (
        jax.ShapeDtypeStruct((snaps * modes, delays, width), f32),
        jax.ShapeDtypeStruct((2, 1, share_rows, width), f32),
    )
    rotated, grams = pl.pallas_call(
        functools.partial(kernel, sizes),
        out_shape=out_shape,
        in_specs=[hbm, hbm, hbm],
        out_specs=(hbm, hbm),
        scratch_shapes=[
            pltpu.SMEM(arrangement.shape, arrangement.dtype),
            pltpu.VMEM(blocks.shape, f32),
            pltpu.VMEM(rotations.shape, f32),
            pltpu.VMEM((width, half), f32),
            pltpu.VMEM((snaps, modes, delays, width), f32),
            pltpu.VMEM((2, modes, delays, width), f32),
            pltpu.VMEM((snaps * modes, delays, width), f32),
            pltpu.VMEM((snaps * modes, delays, width), f32),
            pltpu.VMEM((snaps * modes, delays, half), f32),
            pltpu.VMEM((snaps * modes, delays, half), f32),
            pltpu.VMEM((snaps * modes, delays, half), f32),
            pltpu.VMEM((snaps // GROUPS * modes, delays, half), f32),
            pltpu.VMEM((snaps * modes, delays, width), f32),
            pltpu.VMEM((2, width, width), bf16),
            pltpu.VMEM((2, width, width), bf16),
            pltpu.VMEM((width, half), bf16),
            pltpu.VMEM((width, half), bf16),
            pltpu.VMEM((2, width, 2 * width), f32),
            pltpu.VMEM((2, rows, share_rows, width), f32),
            pltpu.VMEM((2, rows, share_rows, width), f32),
            pltpu.VMEM((2, 1, share_rows, width), f32),
            pltpu.SemaphoreType.DMA((3,)),
            pltpu.SemaphoreType.DMA,
            pltpu.SemaphoreType.DMA((GROUPS,)),
            pltpu.SemaphoreType.DMA,
            pltpu.SemaphoreType.DMA((GROUPS,)),
            pltpu.SemaphoreType.DMA,
            pltpu.SemaphoreType.DMA,
            pltpu.SemaphoreType.DMA,
            pltpu.SemaphoreType.DMA((GROUPS,)),
            pltpu.SemaphoreType.DMA,
            pltpu.SemaphoreType.DMA,
            pltpu.SemaphoreType.DMA,
            pltpu.SemaphoreType.DMA((2,)),
            pltpu.SemaphoreType.DMA((2, rows)),
            pltpu.SemaphoreType.DMA((2, rows)),
        ],
        compiler_params=pltpu.CompilerParams(
            collective_id=0, has_side_effects=True, vmem_limit_bytes=60 * 1024 * 1024
        ),
        name="rounds",
    )(arrangement, blocks, rotations)
    return pl.pallas_call(
        write_results,
        out_shape=out_shape,
        in_specs=[hbm, hbm],
        out_specs=(hbm, hbm),
        scratch_shapes=[
            pltpu.VMEM(out_shape[0].shape, f32),
            pltpu.VMEM(out_shape[1].shape, f32),
            pltpu.SemaphoreType.DMA((9,)),
            pltpu.SemaphoreType.DMA((9,)),
        ],
        compiler_params=pltpu.CompilerParams(vmem_limit_bytes=60 * 1024 * 1024),
        name="write_results",
    )(rotated, grams)


def solution(mesh):
    placed = (P("snap", "row", None), P(), P(None, "snap", None, None))
    return jax.shard_map(
        body,
        mesh=mesh,
        in_specs=placed,
        out_specs=(P(None, "row", "snap"), P(None, "snap", "row", None)),
        check_vma=False,
    )
```

```python
import functools

import jax
import jax.numpy as jnp
from jax import lax
from jax.experimental import pallas as pl
from jax.experimental.pallas import tpu as pltpu
from jax.sharding import PartitionSpec as P

MESH = pl.DeviceIdType.MESH
GROUPS = 8


def split(value):
    high = value.astype(jnp.bfloat16)
    low = (value - high.astype(jnp.float32)).astype(jnp.bfloat16)
    return high, low


def dot(left, right):
    return jnp.dot(left, right, preferred_element_type=jnp.float32)


def dot_rows(left, right):
    return lax.dot_general(left, right, (((0,), (0,)), ((), ())), preferred_element_type=jnp.float32)


def kernel(
    sizes,
    order_hbm,
    x_hbm,
    rot_hbm,
    out_ref,
    gram_out,
    order_ref,
    x_ref,
    rot_ref,
    rot_before,
    stage,
    extra_stage,
    blocks,
    extra,
    first,
    second,
    arrived,
    result,
    rot_high,
    rot_low,
    before_high,
    before_low,
    sums,
    shares,
    share_in,
    gram_ref,
    load_sem,
    a2a_send,
    a2a_recv,
    extra_send,
    extra_recv,
    before_send,
    before_recv,
    next_send,
    next_recv,
    out_sem,
    gram_sem,
    share_send,
    share_recv,
    uppers_in,
    all_in,
    rows_in,
    rows_all_in,
):
    snaps, rows, modes, delays, width = sizes
    half = width // 2
    per_group = snaps // GROUPS
    group_modes = modes * per_group
    group_rows = group_modes * delays
    share_rows = width // rows
    scale = 1.0 / float(modes * snaps * delays * rows)

    me = lax.axis_index("snap")
    row = lax.axis_index("row")
    my_group = me // per_group
    after = (me + 1) % snaps
    run = snaps // 2
    is_head = me % run == 0
    is_last = me % run == run - 1

    loads = [
        pltpu.make_async_copy(order_hbm, order_ref, load_sem.at[0]),
        pltpu.make_async_copy(x_hbm, x_ref, load_sem.at[1]),
        pltpu.make_async_copy(rot_hbm, rot_ref, load_sem.at[2]),
    ]
    for load in loads:
        load.start()

    high_part = me // run
    in_low = high_part == 0
    in_high = high_part == 1
    across = (me + run) % snaps
    barrier = pltpu.get_barrier_semaphore()

    def signal(semaphore, snap, to_row):
        pl.semaphore_signal(
            semaphore, inc=1, device_id={"snap": snap, "row": to_row}, device_id_type=MESH
        )

    @pl.when(in_low)
    def _():
        @pl.loop(1, run)
        def _(i):
            signal(barrier, (me + i) % run, row)

        for i in range(1, rows):
            signal(barrier, me, (row + i) % rows)

    before_copy = pltpu.make_async_remote_copy(
        src_ref=rot_ref.at[0, 0, :, pl.ds(half, half)],
        dst_ref=rot_before,
        send_sem=before_send,
        recv_sem=before_recv,
        device_id={"snap": after, "row": row},
        device_id_type=MESH,
    )

    @pl.when(in_low)
    def _():
        pl.semaphore_wait(barrier, run - 1 + rows - 1)
        signal(barrier, across, row)

    @pl.when(in_high)
    def _():
        pl.semaphore_wait(barrier, 1)

        @pl.loop(0, run)
        def _(i):
            signal(uppers_in, (me + i) % run, row)

    for load in loads:
        load.wait()

    @pl.when(jnp.logical_and(in_high, is_last))
    def _():
        before_copy.start()

    def send_blocks(d):
        stage[d, :, :, :half] = x_ref[:, order_ref[2 * d]]
        stage[d, :, :, half:] = x_ref[:, order_ref[2 * d + 1]]
        pltpu.make_async_remote_copy(
            src_ref=stage.at[d],
            dst_ref=blocks.at[pl.ds(me * modes, modes)],
            send_sem=a2a_send,
            recv_sem=a2a_recv.at[my_group],
            device_id={"snap": d, "row": row},
            device_id_type=MESH,
        ).start()

        @pl.when(d % run == 0)
        def _():
            send_extra(d)

    def send_extra(head):
        before = (head + snaps - 1) % snaps
        place = head // run
        extra_stage[place, :, :, :half] = x_ref[:, order_ref[2 * before]]
        extra_stage[place, :, :, half:] = x_ref[:, order_ref[2 * before + 1]]
        pltpu.make_async_remote_copy(
            src_ref=extra_stage.at[place],
            dst_ref=extra.at[pl.ds(me * modes, modes)],
            send_sem=extra_send,
            recv_sem=extra_recv.at[my_group],
            device_id={"snap": head, "row": row},
            device_id_type=MESH,
        ).start()

    ys = GROUPS // 2
    my_y = my_group % ys
    my_place = me % per_group

    def place_at(k, j):
        return ((my_y + k) % ys) * per_group + (my_place + j) % per_group

    def send_part(k, j, part):
        to = part * run + place_at(k, j)

        @pl.when(to != me)
        def _():
            send_blocks(to)

    @pl.loop(0, jnp.where(in_low, ys, 1))
    def _(k):
        @pl.loop(0, per_group)
        def _(j):
            send_part(k, j, 0)

    @pl.when(in_low)
    def _():
        pl.semaphore_wait(uppers_in, run)
        signal(all_in, across, row)
        for i in range(1, rows):
            signal(rows_in, me, (row + i) % rows)

        @pl.when(is_last)
        def _():
            before_copy.start()

    @pl.when(in_high)
    def _():
        pl.semaphore_wait(all_in, 1)

    @pl.loop(0, ys)
    def _(k):
        @pl.loop(0, per_group)
        def _(j):
            @pl.when(jnp.logical_and(in_high, k > 0))
            def _():
                send_part(k, j, 0)

            send_part(k, j, 1)

    @pl.when(in_low)
    def _():
        pl.semaphore_wait(rows_in, rows - 1)
        signal(rows_all_in, across, row)

    stage[me, :, :, :half] = x_ref[:, order_ref[2 * me]]
    stage[me, :, :, half:] = x_ref[:, order_ref[2 * me + 1]]
    blocks[pl.ds(me * modes, modes)] = stage[me]


    @pl.when(is_head)
    def _():
        before = (me + snaps - 1) % snaps
        extra[pl.ds(me * modes, modes), :, :half] = x_ref[:, order_ref[2 * before]]
        extra[pl.ds(me * modes, modes), :, half:] = x_ref[:, order_ref[2 * before + 1]]

    for r in range(2):
        high, low = split(rot_ref[r, 0])
        rot_high[r] = high
        rot_low[r] = low
    sums[...] = jnp.zeros_like(sums)

    def wait_group(buffer, sems, group):
        whole = buffer.at[pl.ds(0, group_modes)]
        part = buffer.at[pl.ds(0, group_modes - modes)]

        @pl.when(group == my_group)
        def _():
            pltpu.make_async_copy(part, part, sems.at[group]).wait()

        @pl.when(group != my_group)
        def _():
            pltpu.make_async_copy(whole, whole, sems.at[group]).wait()

    def turn(r, matrix):
        high, low = split(matrix)
        return dot(high, rot_high[r]) + (dot(high, rot_low[r]) + dot(low, rot_high[r]))

    def add_gram(r, turned):
        high, low = split(turned)
        sums[r, :, :width] += dot_rows(high, high)
        sums[r, :, width:] += dot_rows(high, low)

    def send_next(group):
        span = pl.ds(group * group_modes, group_modes)
        return pltpu.make_async_remote_copy(
            src_ref=second.at[span],
            dst_ref=arrived.at[span],
            send_sem=next_send,
            recv_sem=next_recv.at[group],
            device_id={"snap": after, "row": row},
            device_id_type=MESH,
        )

    def group_at(k, turned_by):
        part = (high_part + k // ys) % 2
        return part * ys + (my_y + ys - (k + turned_by) % ys) % ys

    def round_one(k):
        group = group_at(k, 0)
        span = pl.ds(group * group_modes, group_modes)
        wait_group(blocks, a2a_recv, group)
        turned = turn(0, blocks[span].reshape(group_rows, width))
        first[span] = turned[:, :half].reshape(group_modes, delays, half)
        second[span] = turned[:, half:].reshape(group_modes, delays, half)

        @pl.when(jnp.logical_not(is_last))
        def _():
            send_next(group).start()

        add_gram(0, turned)

    wraps = jnp.where(jnp.logical_and(my_place == 0, jnp.logical_not(is_head)), 1, 0)

    def round_two(k):
        @pl.when(jnp.logical_and(is_head, k == 0))
        def _():
            before_copy.wait_recv()
            high, low = split(rot_before[...])
            before_high[...] = high
            before_low[...] = low

        group = group_at(k, wraps)
        span = pl.ds(group * group_modes, group_modes)

        @pl.when(jnp.logical_not(is_head))
        def _():
            send_next(group).wait_recv()

        @pl.when(is_head)
        def _():
            wait_group(extra, extra_recv, group)
            high, low = split(extra[span].reshape(group_rows, width))
            turned = dot(high, before_high[...]) + (
                dot(high, before_low[...]) + dot(low, before_high[...])
            )
            arrived[span] = turned.reshape(group_modes, delays, half)

        matrix = jnp.concatenate([first[span], arrived[span]], axis=2)
        turned = turn(1, matrix.reshape(group_rows, width))
        result[span] = turned.reshape(group_modes, delays, width)
        pltpu.make_async_copy(result.at[span], out_ref.at[span], out_sem).start()
        add_gram(1, turned)

    def finish(r):
        cross = sums[r, :, width:]
        total = (sums[r, :, :width] + (cross + cross.T)) * scale
        shares[r] = total.reshape(rows, share_rows, width)
        for i in range(1, rows):
            share_copy(r, i).start()

    def share_copy(r, i):
        to = (row + i) % rows
        return pltpu.make_async_remote_copy(
            src_ref=shares.at[r, to],
            dst_ref=share_in.at[r, i],
            send_sem=share_send.at[r, i],
            recv_sem=share_recv.at[r, i],
            device_id={"snap": me, "row": to},
            device_id_type=MESH,
        )

    def collect(r):
        for i in range(1, rows):
            share_copy(r, i).wait()
        total = shares[r, row]
        for i in range(1, rows):
            total = total + share_in[r, i]
        gram_ref[r, 0] = total
        pltpu.make_async_copy(gram_ref.at[r], gram_out.at[r], gram_sem.at[r]).start()

    round_one(0)

    @pl.loop(1, GROUPS)
    def _(k):
        round_one(k)
        round_two(k - 1)

    @pl.when(in_high)
    def _():
        pl.semaphore_wait(rows_all_in, 1)

    finish(0)
    round_two(GROUPS - 1)
    finish(1)
    collect(0)
    everything = stage.at[pl.ds(0, snaps - 1)]
    pltpu.make_async_copy(everything, everything, a2a_send).wait()
    two = stage.at[pl.ds(0, 2)]
    one = stage.at[0]

    @pl.when(is_head)
    def _():
        pltpu.make_async_copy(one, one, extra_send).wait()

    @pl.when(jnp.logical_not(is_head))
    def _():
        pltpu.make_async_copy(two, two, extra_send).wait()

    @pl.when(is_last)
    def _():
        before_copy.wait_send()

    @pl.when(jnp.logical_not(is_last))
    def _():
        pltpu.make_async_copy(second, second, next_send).wait()

    pltpu.make_async_copy(result, out_ref, out_sem).wait()
    collect(1)
    for r in range(2):
        pltpu.make_async_copy(gram_ref.at[r], gram_out.at[r], gram_sem.at[r]).wait()


def write_results(out_from, gram_from, out_ref, gram_ref, out_held, gram_held, in_sem, out_sem):
    pieces = in_sem.shape[0] - 1
    length = out_ref.shape[0] // pieces
    spans = [pl.ds(i * length, length) for i in range(pieces)]
    steps = [(out_from.at[span], out_held.at[span], out_ref.at[span]) for span in spans]
    steps.append((gram_from, gram_held, gram_ref))
    loads = [pltpu.make_async_copy(a, b, in_sem.at[i]) for i, (a, b, _) in enumerate(steps)]
    stores = [pltpu.make_async_copy(b, c, out_sem.at[i]) for i, (_, b, c) in enumerate(steps)]
    for load in loads:
        load.start()
    for load, store in zip(loads, stores):
        load.wait()
        store.start()
    for store in stores:
        store.wait()


def body(delay_matrix, arrangement, rotations):
    modes, delays, columns = delay_matrix.shape
    snaps = lax.axis_size("snap")
    rows = lax.axis_size("row")
    width = columns // snaps
    half = width // 2
    share_rows = width // rows
    sizes = (snaps, rows, modes, delays, width)
    f32, bf16 = jnp.float32, jnp.bfloat16
    blocks = delay_matrix.reshape(modes, delays, 2 * snaps, half).transpose(0, 2, 1, 3)
    hbm = pl.BlockSpec(memory_space=pltpu.HBM)
    out_shape = (
        jax.ShapeDtypeStruct((snaps * modes, delays, width), f32),
        jax.ShapeDtypeStruct((2, 1, share_rows, width), f32),
    )
    rotated, grams = pl.pallas_call(
        functools.partial(kernel, sizes),
        out_shape=out_shape,
        in_specs=[hbm, hbm, hbm],
        out_specs=(hbm, hbm),
        scratch_shapes=[
            pltpu.SMEM(arrangement.shape, arrangement.dtype),
            pltpu.VMEM(blocks.shape, f32),
            pltpu.VMEM(rotations.shape, f32),
            pltpu.VMEM((width, half), f32),
            pltpu.VMEM((snaps, modes, delays, width), f32),
            pltpu.VMEM((2, modes, delays, width), f32),
            pltpu.VMEM((snaps * modes, delays, width), f32),
            pltpu.VMEM((snaps * modes, delays, width), f32),
            pltpu.VMEM((snaps * modes, delays, half), f32),
            pltpu.VMEM((snaps * modes, delays, half), f32),
            pltpu.VMEM((snaps * modes, delays, half), f32),
            pltpu.VMEM((snaps * modes, delays, width), f32),
            pltpu.VMEM((2, width, width), bf16),
            pltpu.VMEM((2, width, width), bf16),
            pltpu.VMEM((width, half), bf16),
            pltpu.VMEM((width, half), bf16),
            pltpu.VMEM((2, width, 2 * width), f32),
            pltpu.VMEM((2, rows, share_rows, width), f32),
            pltpu.VMEM((2, rows, share_rows, width), f32),
            pltpu.VMEM((2, 1, share_rows, width), f32),
            pltpu.SemaphoreType.DMA((3,)),
            pltpu.SemaphoreType.DMA,
            pltpu.SemaphoreType.DMA((GROUPS,)),
            pltpu.SemaphoreType.DMA,
            pltpu.SemaphoreType.DMA((GROUPS,)),
            pltpu.SemaphoreType.DMA,
            pltpu.SemaphoreType.DMA,
            pltpu.SemaphoreType.DMA,
            pltpu.SemaphoreType.DMA((GROUPS,)),
            pltpu.SemaphoreType.DMA,
            pltpu.SemaphoreType.DMA((2,)),
            pltpu.SemaphoreType.DMA((2, rows)),
            pltpu.SemaphoreType.DMA((2, rows)),
            pltpu.SemaphoreType.REGULAR,
            pltpu.SemaphoreType.REGULAR,
            pltpu.SemaphoreType.REGULAR,
            pltpu.SemaphoreType.REGULAR,
        ],
        compiler_params=pltpu.CompilerParams(
            collective_id=0, has_side_effects=True, vmem_limit_bytes=60 * 1024 * 1024
        ),
        name="rounds",
    )(arrangement, blocks, rotations)
    return pl.pallas_call(
        write_results,
        out_shape=out_shape,
        in_specs=[hbm, hbm],
        out_specs=(hbm, hbm),
        scratch_shapes=[
            pltpu.VMEM(out_shape[0].shape, f32),
            pltpu.VMEM(out_shape[1].shape, f32),
            pltpu.SemaphoreType.DMA((9,)),
            pltpu.SemaphoreType.DMA((9,)),
        ],
        compiler_params=pltpu.CompilerParams(vmem_limit_bytes=60 * 1024 * 1024),
        name="write_results",
    )(rotated, grams)


def solution(mesh):
    placed = (P("snap", "row", None), P(), P(None, "snap", None, None))
    return jax.shard_map(
        body,
        mesh=mesh,
        in_specs=placed,
        out_specs=(P(None, "row", "snap"), P(None, "snap", "row", None)),
        check_vma=False,
    )
```

```python
import functools

import jax
import jax.numpy as jnp
from jax import lax
from jax.experimental import pallas as pl
from jax.experimental.pallas import tpu as pltpu
from jax.sharding import PartitionSpec as P

MESH = pl.DeviceIdType.MESH
BATCH = 4
EARLY = 8
HELPER = 3
GROUPS = 8


def split(value):
    high = value.astype(jnp.bfloat16)
    low = (value - high.astype(jnp.float32)).astype(jnp.bfloat16)
    return high, low


def dot(left, right):
    return jnp.dot(left, right, preferred_element_type=jnp.float32)


def dot_rows(left, right):
    return lax.dot_general(left, right, (((0,), (0,)), ((), ())), preferred_element_type=jnp.float32)


def kernel(
    sizes,
    order_hbm,
    x_hbm,
    rot_hbm,
    out_ref,
    gram_ref,
    order_ref,
    x_ref,
    rot_ref,
    rot_before,
    stage,
    over,
    landed,
    rot_landed,
    blocks,
    extra,
    helped,
    first,
    second,
    arrived,
    rot_high,
    rot_low,
    before_high,
    before_low,
    shares,
    share_in,
    load_sem,
    a2a_send,
    a2a_recv,
    extra_send,
    extra_recv,
    before_send,
    before_recv,
    over_send,
    over_recv,
    rot_send,
    rot_recv,
    help_send,
    partner_in,
    partners_in,
    half_in,
    rows_in,
    rows_all_in,
    next_send,
    next_recv,
    share_send,
    share_recv,
):
    snaps, rows, modes, delays, width = sizes
    half = width // 2
    per_group = snaps // GROUPS
    group_modes = modes * per_group
    group_rows = group_modes * delays
    share_rows = width // rows
    scale = 1.0 / float(modes * snaps * delays * rows)

    me = lax.axis_index("snap")
    row = lax.axis_index("row")
    my_group = me // per_group
    after = (me + 1) % snaps
    run = snaps // 2
    is_head = me % run == 0
    is_last = me % run == run - 1

    loads = [
        pltpu.make_async_copy(order_hbm, order_ref, load_sem.at[0]),
        pltpu.make_async_copy(x_hbm, x_ref, load_sem.at[1]),
        pltpu.make_async_copy(rot_hbm, rot_ref, load_sem.at[2]),
    ]
    for load in loads:
        load.start()

    barrier = pltpu.get_barrier_semaphore()
    high_part = me // run
    in_low, in_high = high_part == 0, high_part == 1
    my_head = high_part * run
    across = (me + run) % snaps
    my_span = pl.ds(me * modes, modes)
    across_span = pl.ds(across * modes, modes)
    across_group = across // per_group
    ys = GROUPS // 2
    my_y = my_group % ys
    my_place = me % per_group

    def signal(semaphore, snap, to_row):
        pl.semaphore_signal(
            semaphore, inc=1, device_id={"snap": snap, "row": to_row}, device_id_type=MESH
        )

    def remote(source, target, send, recv, snap):
        return pltpu.make_async_remote_copy(
            src_ref=source,
            dst_ref=target,
            send_sem=send,
            recv_sem=recv,
            device_id={"snap": snap, "row": row},
            device_id_type=MESH,
        )

    def place_at(i):
        k, j = i // per_group, i % per_group
        return ((my_y + k) % ys) * per_group + (my_place + j) % per_group

    def take(target, d):
        target[:, :, :half] = x_ref[:, order_ref[2 * d]]
        target[:, :, half:] = x_ref[:, order_ref[2 * d + 1]]

    def cross_copy(batch):
        span = pl.ds(batch * BATCH, BATCH)
        return remote(over.at[span], landed.at[span], over_send, over_recv.at[batch], across)

    def cross_extra():
        return remote(over.at[EARLY], landed.at[EARLY], over_send, over_recv.at[batches], across)

    def send_across():
        @pl.when(is_last)
        def _():
            rot_across.start()

        @pl.loop(0, batches)
        def _(batch):
            @pl.loop(0, BATCH)
            def _(j):
                i = batch * BATCH + j
                take(over.at[i], (run - my_head) + place_at(i))

            cross_copy(batch).start()

            @pl.when(batch == 1)
            def _():
                take(over.at[EARLY], (run - my_head + snaps - 1) % snaps)
                cross_extra().start()

    helper = my_head + my_y * per_group + HELPER
    is_helper = my_place == HELPER
    place_span = pl.ds(my_place * modes, modes)
    other_pair = (my_head + snaps - 1) % snaps

    def send_inside(i):
        d = my_head + place_at(i)
        take(stage.at[i], d)
        remote(stage.at[i], blocks.at[my_span], a2a_send, a2a_recv.at[my_group], d).start()

        @pl.when(d == helper)
        def _():
            take(stage.at[0], other_pair)
            remote(
                stage.at[0], extra.at[0, place_span], extra_send, extra_recv.at[0], helper
            ).start()

    def send_direct(i):
        d = run - my_head + place_at(i)
        take(stage.at[run + i], d)
        remote(stage.at[run + i], blocks.at[my_span], a2a_send, a2a_recv.at[my_group], d).start()

    batches = EARLY // BATCH
    rot_across = remote(
        rot_ref.at[0, 0, :, pl.ds(half, half)], rot_landed, before_send, rot_recv, across
    )
    rot_on = [
        remote(rot_landed, rot_before, rot_send.at[y], before_recv, my_head + y * per_group + HELPER)
        for y in range(ys)
    ]

    def prepare():
        take(blocks.at[my_span], me)

        @pl.when(is_helper)
        def _():
            take(extra.at[0, place_span], other_pair)

        for r in range(2):
            high, low = split(rot_ref[r, 0])
            rot_high[r] = high
            rot_low[r] = low
        shares[...] = jnp.zeros_like(shares)

    @pl.when(in_low)
    def _():
        signal(barrier, across, row)

        @pl.loop(1, run)
        def _(i):
            signal(barrier, (me + i) % run, row)

        for i in range(1, rows):
            signal(barrier, me, (row + i) % rows)

        for load in loads:
            load.wait()
        pl.semaphore_wait(barrier, run - 1 + rows - 1)
        pl.semaphore_wait(partner_in, 1)

        @pl.loop(1, run)
        def _(i):
            signal(partners_in, (me + i) % run, row)

        send_across()

        @pl.loop(1, run)
        def _(i):
            send_inside(i)

        pl.semaphore_wait(partners_in, run - 1)
        signal(half_in, across, row)
        for i in range(1, rows):
            signal(rows_in, me, (row + i) % rows)

        @pl.loop(EARLY, run)
        def _(i):
            send_direct(i)

        prepare()
        pl.semaphore_wait(rows_in, rows - 1)
        signal(rows_all_in, across, row)

    @pl.when(in_high)
    def _():
        pl.semaphore_wait(barrier, 1)
        signal(partner_in, across, row)
        for load in loads:
            load.wait()
        send_across()
        prepare()
        pl.semaphore_wait(half_in, 1)

        @pl.loop(1, run)
        def _(i):
            @pl.when(i >= EARLY)
            def _():
                send_direct(i)

            send_inside(i)


    def pass_on(batch):
        cross_copy(batch).wait_recv()

        @pl.loop(0, BATCH)
        def _(j):
            i = batch * BATCH + j
            d = my_head + place_at(i)

            @pl.when(i == 0)
            def _():
                blocks[across_span] = landed[0]

            @pl.when(i > 0)
            def _():
                remote(
                    landed.at[i], blocks.at[across_span], a2a_send, a2a_recv.at[across_group], d
                ).start()

    def pass_extra_on():
        cross_extra().wait_recv()

        @pl.when(is_helper)
        def _():
            extra[1, place_span] = landed[EARLY]

        @pl.when(jnp.logical_not(is_helper))
        def _():
            remote(
                landed.at[EARLY], extra.at[1, place_span], extra_send, extra_recv.at[1], helper
            ).start()

    def help_first(side):
        group = (my_group, across_group)[side]
        part = extra.at[side, pl.ds(0, group_modes - modes)]
        pltpu.make_async_copy(part, part, extra_recv.at[side]).wait()
        high, low = split(extra[side].reshape(group_rows, width))
        other = dot(high, before_high[...]) + (
            dot(high, before_low[...]) + dot(low, before_high[...])
        )
        helped[side] = other.reshape(group_modes, delays, half)
        help_copy(side, group).start()

    def help_copy(side, group):
        span = pl.ds(group * group_modes, group_modes)
        return remote(
            helped.at[side], arrived.at[span], help_send.at[side], next_recv.at[group], my_head
        )

    def pass_on_all():
        @pl.when(is_last)
        def _():
            rot_across.wait_recv()
            for copy in rot_on:
                copy.start()

        for batch in range(batches):
            pass_on(batch)
        pass_extra_on()

    def wait_group(buffer, sems, group):
        whole = buffer.at[pl.ds(0, group_modes)]
        part = buffer.at[pl.ds(0, group_modes - modes)]

        @pl.when(group % ys == my_y)
        def _():
            pltpu.make_async_copy(part, part, sems.at[group]).wait()

        @pl.when(group % ys != my_y)
        def _():
            pltpu.make_async_copy(whole, whole, sems.at[group]).wait()

    def turn(r, matrix):
        high, low = split(matrix)
        return dot(high, rot_high[r]) + (dot(high, rot_low[r]) + dot(low, rot_high[r]))

    def add_gram(r, turned):
        high, low = split(turned)
        part = dot_rows(high, high) + (dot_rows(high, low) + dot_rows(low, high))
        shares[r] += part.reshape(rows, share_rows, width)

    def send_next(group):
        span = pl.ds(group * group_modes, group_modes)
        return pltpu.make_async_remote_copy(
            src_ref=second.at[span],
            dst_ref=arrived.at[span],
            send_sem=next_send,
            recv_sem=next_recv.at[group],
            device_id={"snap": after, "row": row},
            device_id_type=MESH,
        )

    def group_of(crossing, k):
        return (high_part + crossing) % 2 * ys + (my_y + ys - k % ys) % ys

    def in_order(i):
        crossing = jnp.where(jnp.logical_or(i == 2, i >= 5), 1, 0)
        before = jnp.where(i >= 5, i - 4, jnp.where(i == 2, 0, jnp.where(i > 2, i - 1, i)))
        return crossing, before

    def round_one(k):
        group = group_of(*in_order(k))
        span = pl.ds(group * group_modes, group_modes)
        wait_group(blocks, a2a_recv, group)
        turned = turn(0, blocks[span].reshape(group_rows, width))
        first[span] = turned[:, :half].reshape(group_modes, delays, half)
        second[span] = turned[:, half:].reshape(group_modes, delays, half)

        @pl.when(jnp.logical_not(is_last))
        def _():
            send_next(group).start()

        add_gram(0, turned)

    wraps = jnp.logical_and(my_place == 0, jnp.logical_not(is_head))

    def round_two(k):
        crossing, step = in_order(k)
        group = jnp.where(wraps, group_of(k // ys, k % ys + 1), group_of(crossing, step))
        span = pl.ds(group * group_modes, group_modes)

        send_next(group).wait_recv()
        matrix = jnp.concatenate([first[span], arrived[span]], axis=2)
        turned = turn(1, matrix.reshape(group_rows, width))
        out_ref[span] = turned.reshape(group_modes, delays, width)
        add_gram(1, turned)

    def finish(r):
        for i in range(1, rows):
            share_copy(r, i).start()

    def share_copy(r, i):
        to = (row + i) % rows
        return pltpu.make_async_remote_copy(
            src_ref=shares.at[r, to],
            dst_ref=share_in.at[r, i],
            send_sem=share_send.at[r, i],
            recv_sem=share_recv.at[r, i],
            device_id={"snap": me, "row": to},
            device_id_type=MESH,
        )

    def collect(r):
        for i in range(1, rows):
            share_copy(r, i).wait()
        total = shares[r, row]
        for i in range(1, rows):
            total = total + share_in[r, i]
        gram_ref[r, 0] = total * scale

    pass_on_all()

    @pl.loop(0, GROUPS)
    def _(k):
        round_one(k)

        @pl.when(jnp.logical_and(is_helper, k == 3))
        def _():
            rot_on[0].wait_recv()
            high, low = split(rot_before[...])
            before_high[...] = high
            before_low[...] = low
            for side in range(2):
                help_first(side)

        @pl.loop(jnp.where(k == 6, 4, 0), jnp.where(k == 5, 4, jnp.where(k == 6, 6, 0)))
        def _(j):
            round_two(j)

    @pl.when(in_high)
    def _():
        pl.semaphore_wait(rows_all_in, 1)

    finish(0)

    @pl.loop(GROUPS - 2, GROUPS)
    def _(j):
        round_two(j)

    finish(1)
    collect(0)
    sent = blocks.at[pl.ds(0, 2 * (run - 1) * modes)]
    pltpu.make_async_copy(sent, sent, a2a_send).wait()
    pltpu.make_async_copy(over, over, over_send).wait()

    @pl.when(jnp.logical_not(is_helper))
    def _():
        two = stage.at[pl.ds(0, 2)]
        pltpu.make_async_copy(two, two, extra_send).wait()

    @pl.when(is_helper)
    def _():
        for side in range(2):
            help_copy(side, (my_group, across_group)[side]).wait_send()

    @pl.when(is_last)
    def _():
        rot_across.wait_send()
        for copy in rot_on:
            copy.wait_send()

    @pl.when(jnp.logical_not(is_last))
    def _():
        pltpu.make_async_copy(second, second, next_send).wait()

    collect(1)


def write_results(out_from, gram_from, out_ref, gram_ref, sems):
    copies = [
        pltpu.make_async_copy(out_from, out_ref, sems.at[0]),
        pltpu.make_async_copy(gram_from, gram_ref, sems.at[1]),
    ]
    for copy in copies:
        copy.start()
    for copy in copies:
        copy.wait()


def body(delay_matrix, arrangement, rotations):
    modes, delays, columns = delay_matrix.shape
    snaps = lax.axis_size("snap")
    rows = lax.axis_size("row")
    width = columns // snaps
    half = width // 2
    share_rows = width // rows
    sizes = (snaps, rows, modes, delays, width)
    f32, bf16 = jnp.float32, jnp.bfloat16
    blocks = delay_matrix.reshape(modes, delays, 2 * snaps, half).transpose(0, 2, 1, 3)
    hbm = pl.BlockSpec(memory_space=pltpu.HBM)
    vmem = pl.BlockSpec(memory_space=pltpu.VMEM)
    out_shape = (
        jax.ShapeDtypeStruct((snaps * modes, delays, width), f32),
        jax.ShapeDtypeStruct((2, 1, share_rows, width), f32),
    )
    rotated, grams = pl.pallas_call(
        functools.partial(kernel, sizes),
        out_shape=tuple(pltpu.VMEM(s.shape, s.dtype) for s in out_shape),
        in_specs=[hbm, hbm, hbm],
        out_specs=(vmem, vmem),
        scratch_shapes=[
            pltpu.SMEM(arrangement.shape, arrangement.dtype),
            pltpu.VMEM(blocks.shape, f32),
            pltpu.VMEM(rotations.shape, f32),
            pltpu.VMEM((width, half), f32),
            pltpu.VMEM((snaps, modes, delays, width), f32),
            pltpu.VMEM((EARLY + 1, modes, delays, width), f32),
            pltpu.VMEM((EARLY + 1, modes, delays, width), f32),
            pltpu.VMEM((width, half), f32),
            pltpu.VMEM((snaps * modes, delays, width), f32),
            pltpu.VMEM((2, snaps // GROUPS * modes, delays, width), f32),
            pltpu.VMEM((2, snaps // GROUPS * modes, delays, half), f32),
            pltpu.VMEM((snaps * modes, delays, half), f32),
            pltpu.VMEM((snaps * modes, delays, half), f32),
            pltpu.VMEM((snaps * modes, delays, half), f32),
            pltpu.VMEM((2, width, width), bf16),
            pltpu.VMEM((2, width, width), bf16),
            pltpu.VMEM((width, half), bf16),
            pltpu.VMEM((width, half), bf16),
            pltpu.VMEM((2, rows, share_rows, width), f32),
            pltpu.VMEM((2, rows, share_rows, width), f32),
            pltpu.SemaphoreType.DMA((3,)),
            pltpu.SemaphoreType.DMA,
            pltpu.SemaphoreType.DMA((GROUPS,)),
            pltpu.SemaphoreType.DMA,
            pltpu.SemaphoreType.DMA((2,)),
            pltpu.SemaphoreType.DMA,
            pltpu.SemaphoreType.DMA,
            pltpu.SemaphoreType.DMA,
            pltpu.SemaphoreType.DMA((EARLY // BATCH + 1,)),
            pltpu.SemaphoreType.DMA((GROUPS // 2,)),
            pltpu.SemaphoreType.DMA,
            pltpu.SemaphoreType.DMA((2,)),
            pltpu.SemaphoreType.REGULAR,
            pltpu.SemaphoreType.REGULAR,
            pltpu.SemaphoreType.REGULAR,
            pltpu.SemaphoreType.REGULAR,
            pltpu.SemaphoreType.REGULAR,
            pltpu.SemaphoreType.DMA,
            pltpu.SemaphoreType.DMA((GROUPS,)),
            pltpu.SemaphoreType.DMA((2, rows)),
            pltpu.SemaphoreType.DMA((2, rows)),
        ],
        compiler_params=pltpu.CompilerParams(
            collective_id=0, has_side_effects=True, vmem_limit_bytes=60 * 1024 * 1024
        ),
        name="rounds",
    )(arrangement, blocks, rotations)
    return pl.pallas_call(
        write_results,
        out_shape=out_shape,
        in_specs=[vmem, vmem],
        out_specs=(hbm, hbm),
        scratch_shapes=[pltpu.SemaphoreType.DMA((2,))],
        name="write_results",
    )(
        pltpu.with_memory_space_constraint(rotated, pltpu.VMEM),
        pltpu.with_memory_space_constraint(grams, pltpu.VMEM),
    )


def solution(mesh):
    placed = (P("snap", "row", None), P(), P(None, "snap", None, None))
    return jax.shard_map(
        body,
        mesh=mesh,
        in_specs=placed,
        out_specs=(P(None, "row", "snap"), P(None, "snap", "row", None)),
        check_vma=False,
    )
```

```python
import functools

import jax
import jax.numpy as jnp
from jax import lax
from jax.experimental import pallas as pl
from jax.experimental.pallas import tpu as pltpu
from jax.sharding import PartitionSpec as P

MESH = pl.DeviceIdType.MESH
BATCH = 4
EARLY = 8
HELPER = 3
GROUPS = 8


def split(value):
    high = value.astype(jnp.bfloat16)
    low = (value - high.astype(jnp.float32)).astype(jnp.bfloat16)
    return high, low


def dot(left, right):
    return jnp.dot(left, right, preferred_element_type=jnp.float32)


def dot_rows(left, right):
    return lax.dot_general(left, right, (((0,), (0,)), ((), ())), preferred_element_type=jnp.float32)


def kernel(
    sizes,
    order_hbm,
    x_hbm,
    rot_hbm,
    out_ref,
    gram_ref,
    order_ref,
    x_ref,
    rot_ref,
    rot_before,
    stage,
    over,
    landed,
    rot_landed,
    blocks,
    extra,
    helped,
    first,
    second,
    arrived,
    rot_high,
    rot_low,
    before_high,
    before_low,
    shares,
    share_in,
    load_sem,
    a2a_send,
    a2a_recv,
    extra_send,
    extra_recv,
    before_send,
    before_recv,
    over_send,
    over_recv,
    rot_send,
    rot_recv,
    help_send,
    partner_in,
    partners_in,
    half_in,
    rows_in,
    rows_all_in,
    next_send,
    next_recv,
    share_send,
    share_recv,
):
    snaps, rows, modes, delays, width = sizes
    half = width // 2
    per_group = snaps // GROUPS
    group_modes = modes * per_group
    group_rows = group_modes * delays
    share_rows = width // rows
    scale = 1.0 / float(modes * snaps * delays * rows)

    me = lax.axis_index("snap")
    row = lax.axis_index("row")
    my_group = me // per_group
    after = (me + 1) % snaps
    run = snaps // 2
    is_head = me % run == 0
    is_last = me % run == run - 1

    loads = [
        pltpu.make_async_copy(order_hbm, order_ref, load_sem.at[0]),
        pltpu.make_async_copy(x_hbm, x_ref, load_sem.at[1]),
        pltpu.make_async_copy(rot_hbm, rot_ref, load_sem.at[2]),
    ]
    for load in loads:
        load.start()

    barrier = pltpu.get_barrier_semaphore()
    high_part = me // run
    in_low, in_high = high_part == 0, high_part == 1
    my_head = high_part * run
    across = (me + run) % snaps
    my_span = pl.ds(me * modes, modes)
    across_span = pl.ds(across * modes, modes)
    across_group = across // per_group
    ys = GROUPS // 2
    my_y = my_group % ys
    my_place = me % per_group

    def signal(semaphore, snap, to_row):
        pl.semaphore_signal(
            semaphore, inc=1, device_id={"snap": snap, "row": to_row}, device_id_type=MESH
        )

    def remote(source, target, send, recv, snap):
        return pltpu.make_async_remote_copy(
            src_ref=source,
            dst_ref=target,
            send_sem=send,
            recv_sem=recv,
            device_id={"snap": snap, "row": row},
            device_id_type=MESH,
        )

    def place_at(i):
        k, j = i // per_group, i % per_group
        return ((my_y + k) % ys) * per_group + (my_place + j) % per_group

    def take(target, d):
        target[:, :, :half] = x_ref[:, order_ref[2 * d]]
        target[:, :, half:] = x_ref[:, order_ref[2 * d + 1]]

    def cross_copy(batch):
        span = pl.ds(batch * BATCH, BATCH)
        return remote(over.at[span], landed.at[span], over_send, over_recv.at[batch], across)

    def cross_extra():
        return remote(over.at[EARLY], landed.at[EARLY], over_send, over_recv.at[batches], across)

    def send_across():
        @pl.when(is_last)
        def _():
            rot_across.start()

        @pl.loop(0, batches)
        def _(batch):
            @pl.loop(0, BATCH)
            def _(j):
                i = batch * BATCH + j
                take(over.at[i], (run - my_head) + place_at(i))

            cross_copy(batch).start()

            @pl.when(batch == 1)
            def _():
                take(over.at[EARLY], (run - my_head + snaps - 1) % snaps)
                cross_extra().start()

    helper = my_head + my_y * per_group + HELPER
    is_helper = my_place == HELPER
    place_span = pl.ds(my_place * modes, modes)
    other_pair = (my_head + snaps - 1) % snaps

    def send_inside(i):
        d = my_head + place_at(i)
        take(stage.at[i], d)
        remote(stage.at[i], blocks.at[my_span], a2a_send, a2a_recv.at[my_group], d).start()

        @pl.when(d == helper)
        def _():
            take(stage.at[0], other_pair)
            remote(
                stage.at[0], extra.at[0, place_span], extra_send, extra_recv.at[0], helper
            ).start()

    def send_direct(i):
        d = run - my_head + place_at(i)
        take(stage.at[run + i], d)
        remote(stage.at[run + i], blocks.at[my_span], a2a_send, a2a_recv.at[my_group], d).start()

    batches = EARLY // BATCH
    rot_across = remote(
        rot_ref.at[0, 0, :, pl.ds(half, half)], rot_landed, before_send, rot_recv, across
    )
    rot_on = [
        remote(rot_landed, rot_before, rot_send.at[y], before_recv, my_head + y * per_group + HELPER)
        for y in range(ys)
    ]

    def prepare():
        take(blocks.at[my_span], me)

        @pl.when(is_helper)
        def _():
            take(extra.at[0, place_span], other_pair)

        for r in range(2):
            high, low = split(rot_ref[r, 0])
            rot_high[r] = high
            rot_low[r] = low
        shares[...] = jnp.zeros_like(shares)

    @pl.when(in_low)
    def _():
        signal(barrier, across, row)

        @pl.loop(1, run)
        def _(i):
            signal(barrier, (me + i) % run, row)

        for i in range(1, rows):
            signal(barrier, me, (row + i) % rows)

        for load in loads:
            load.wait()
        pl.semaphore_wait(barrier, run - 1 + rows - 1)
        signal(barrier, across, row)
        pl.semaphore_wait(partner_in, 1)

        @pl.loop(1, run)
        def _(i):
            signal(partners_in, (me + i) % run, row)

        send_across()

        @pl.loop(1, run)
        def _(i):
            send_inside(i)

        pl.semaphore_wait(partners_in, run - 1)
        signal(half_in, across, row)
        for i in range(1, rows):
            signal(rows_in, me, (row + i) % rows)

        @pl.loop(EARLY, run)
        def _(i):
            send_direct(i)

        prepare()
        pl.semaphore_wait(rows_in, rows - 1)
        signal(rows_all_in, across, row)

    @pl.when(in_high)
    def _():
        pl.semaphore_wait(barrier, 1)
        signal(partner_in, across, row)
        for load in loads:
            load.wait()
        send_across()
        pl.semaphore_wait(barrier, 1)

        @pl.loop(EARLY, run)
        def _(i):
            send_direct(i)

        prepare()
        pl.semaphore_wait(half_in, 1)

        @pl.loop(1, run)
        def _(i):
            send_inside(i)


    def pass_on(batch):
        cross_copy(batch).wait_recv()

        @pl.loop(0, BATCH)
        def _(j):
            i = batch * BATCH + j
            d = my_head + place_at(i)

            @pl.when(i == 0)
            def _():
                blocks[across_span] = landed[0]

            @pl.when(i > 0)
            def _():
                remote(
                    landed.at[i], blocks.at[across_span], a2a_send, a2a_recv.at[across_group], d
                ).start()

    def pass_extra_on():
        cross_extra().wait_recv()

        @pl.when(is_helper)
        def _():
            extra[1, place_span] = landed[EARLY]

        @pl.when(jnp.logical_not(is_helper))
        def _():
            remote(
                landed.at[EARLY], extra.at[1, place_span], extra_send, extra_recv.at[1], helper
            ).start()

    def help_first(side):
        group = (my_group, across_group)[side]
        part = extra.at[side, pl.ds(0, group_modes - modes)]
        pltpu.make_async_copy(part, part, extra_recv.at[side]).wait()
        high, low = split(extra[side].reshape(group_rows, width))
        other = dot(high, before_high[...]) + (
            dot(high, before_low[...]) + dot(low, before_high[...])
        )
        helped[side] = other.reshape(group_modes, delays, half)
        help_copy(side, group).start()

    def help_copy(side, group):
        span = pl.ds(group * group_modes, group_modes)
        return remote(
            helped.at[side], arrived.at[span], help_send.at[side], next_recv.at[group], my_head
        )

    def pass_on_all():
        @pl.when(is_last)
        def _():
            rot_across.wait_recv()
            for copy in rot_on:
                copy.start()

        for batch in range(batches):
            pass_on(batch)
        pass_extra_on()

    def wait_group(buffer, sems, group):
        whole = buffer.at[pl.ds(0, group_modes)]
        part = buffer.at[pl.ds(0, group_modes - modes)]

        @pl.when(group % ys == my_y)
        def _():
            pltpu.make_async_copy(part, part, sems.at[group]).wait()

        @pl.when(group % ys != my_y)
        def _():
            pltpu.make_async_copy(whole, whole, sems.at[group]).wait()

    def turn(r, matrix):
        high, low = split(matrix)
        return dot(high, rot_high[r]) + (dot(high, rot_low[r]) + dot(low, rot_high[r]))

    def add_gram(r, turned):
        high, low = split(turned)
        part = dot_rows(high, high) + (dot_rows(high, low) + dot_rows(low, high))
        shares[r] += part.reshape(rows, share_rows, width)

    def send_next(group):
        span = pl.ds(group * group_modes, group_modes)
        return pltpu.make_async_remote_copy(
            src_ref=second.at[span],
            dst_ref=arrived.at[span],
            send_sem=next_send,
            recv_sem=next_recv.at[group],
            device_id={"snap": after, "row": row},
            device_id_type=MESH,
        )

    def group_of(crossing, k):
        return (high_part + crossing) % 2 * ys + (my_y + ys - k % ys) % ys

    def in_order(i):
        crossing = jnp.where(jnp.logical_or(i == 2, i >= 5), 1, 0)
        before = jnp.where(i >= 5, i - 4, jnp.where(i == 2, 0, jnp.where(i > 2, i - 1, i)))
        return crossing, before

    def round_one(k):
        group = group_of(*in_order(k))
        span = pl.ds(group * group_modes, group_modes)
        wait_group(blocks, a2a_recv, group)
        turned = turn(0, blocks[span].reshape(group_rows, width))
        first[span] = turned[:, :half].reshape(group_modes, delays, half)
        second[span] = turned[:, half:].reshape(group_modes, delays, half)

        @pl.when(jnp.logical_not(is_last))
        def _():
            send_next(group).start()

        add_gram(0, turned)

    wraps = jnp.logical_and(my_place == 0, jnp.logical_not(is_head))

    def round_two(k):
        crossing, step = in_order(k)
        group = jnp.where(wraps, group_of(k // ys, k % ys + 1), group_of(crossing, step))
        span = pl.ds(group * group_modes, group_modes)

        send_next(group).wait_recv()
        matrix = jnp.concatenate([first[span], arrived[span]], axis=2)
        turned = turn(1, matrix.reshape(group_rows, width))
        out_ref[span] = turned.reshape(group_modes, delays, width)
        add_gram(1, turned)

    def finish(r):
        for i in range(1, rows):
            share_copy(r, i).start()

    def share_copy(r, i):
        to = (row + i) % rows
        return pltpu.make_async_remote_copy(
            src_ref=shares.at[r, to],
            dst_ref=share_in.at[r, i],
            send_sem=share_send.at[r, i],
            recv_sem=share_recv.at[r, i],
            device_id={"snap": me, "row": to},
            device_id_type=MESH,
        )

    def collect(r):
        for i in range(1, rows):
            share_copy(r, i).wait()
        total = shares[r, row]
        for i in range(1, rows):
            total = total + share_in[r, i]
        gram_ref[r, 0] = total * scale

    pass_on_all()

    @pl.loop(0, GROUPS)
    def _(k):
        round_one(k)

        @pl.when(jnp.logical_and(is_helper, k == 3))
        def _():
            rot_on[0].wait_recv()
            high, low = split(rot_before[...])
            before_high[...] = high
            before_low[...] = low
            for side in range(2):
                help_first(side)

        @pl.loop(jnp.where(k == 6, 4, 0), jnp.where(k == 5, 4, jnp.where(k == 6, 6, 0)))
        def _(j):
            round_two(j)

    @pl.when(in_high)
    def _():
        pl.semaphore_wait(rows_all_in, 1)

    finish(0)

    @pl.loop(GROUPS - 2, GROUPS)
    def _(j):
        round_two(j)

    finish(1)
    collect(0)
    sent = blocks.at[pl.ds(0, 2 * (run - 1) * modes)]
    pltpu.make_async_copy(sent, sent, a2a_send).wait()
    pltpu.make_async_copy(over, over, over_send).wait()

    @pl.when(jnp.logical_not(is_helper))
    def _():
        two = stage.at[pl.ds(0, 2)]
        pltpu.make_async_copy(two, two, extra_send).wait()

    @pl.when(is_helper)
    def _():
        for side in range(2):
            help_copy(side, (my_group, across_group)[side]).wait_send()

    @pl.when(is_last)
    def _():
        rot_across.wait_send()
        for copy in rot_on:
            copy.wait_send()

    @pl.when(jnp.logical_not(is_last))
    def _():
        pltpu.make_async_copy(second, second, next_send).wait()

    collect(1)


def write_results(out_from, gram_from, out_ref, gram_ref, sems):
    copies = [
        pltpu.make_async_copy(out_from, out_ref, sems.at[0]),
        pltpu.make_async_copy(gram_from, gram_ref, sems.at[1]),
    ]
    for copy in copies:
        copy.start()
    for copy in copies:
        copy.wait()


def body(delay_matrix, arrangement, rotations):
    modes, delays, columns = delay_matrix.shape
    snaps = lax.axis_size("snap")
    rows = lax.axis_size("row")
    width = columns // snaps
    half = width // 2
    share_rows = width // rows
    sizes = (snaps, rows, modes, delays, width)
    f32, bf16 = jnp.float32, jnp.bfloat16
    blocks = delay_matrix.reshape(modes, delays, 2 * snaps, half).transpose(0, 2, 1, 3)
    hbm = pl.BlockSpec(memory_space=pltpu.HBM)
    vmem = pl.BlockSpec(memory_space=pltpu.VMEM)
    out_shape = (
        jax.ShapeDtypeStruct((snaps * modes, delays, width), f32),
        jax.ShapeDtypeStruct((2, 1, share_rows, width), f32),
    )
    rotated, grams = pl.pallas_call(
        functools.partial(kernel, sizes),
        out_shape=tuple(pltpu.VMEM(s.shape, s.dtype) for s in out_shape),
        in_specs=[hbm, hbm, hbm],
        out_specs=(vmem, vmem),
        scratch_shapes=[
            pltpu.SMEM(arrangement.shape, arrangement.dtype),
            pltpu.VMEM(blocks.shape, f32),
            pltpu.VMEM(rotations.shape, f32),
            pltpu.VMEM((width, half), f32),
            pltpu.VMEM((snaps, modes, delays, width), f32),
            pltpu.VMEM((EARLY + 1, modes, delays, width), f32),
            pltpu.VMEM((EARLY + 1, modes, delays, width), f32),
            pltpu.VMEM((width, half), f32),
            pltpu.VMEM((snaps * modes, delays, width), f32),
            pltpu.VMEM((2, snaps // GROUPS * modes, delays, width), f32),
            pltpu.VMEM((2, snaps // GROUPS * modes, delays, half), f32),
            pltpu.VMEM((snaps * modes, delays, half), f32),
            pltpu.VMEM((snaps * modes, delays, half), f32),
            pltpu.VMEM((snaps * modes, delays, half), f32),
            pltpu.VMEM((2, width, width), bf16),
            pltpu.VMEM((2, width, width), bf16),
            pltpu.VMEM((width, half), bf16),
            pltpu.VMEM((width, half), bf16),
            pltpu.VMEM((2, rows, share_rows, width), f32),
            pltpu.VMEM((2, rows, share_rows, width), f32),
            pltpu.SemaphoreType.DMA((3,)),
            pltpu.SemaphoreType.DMA,
            pltpu.SemaphoreType.DMA((GROUPS,)),
            pltpu.SemaphoreType.DMA,
            pltpu.SemaphoreType.DMA((2,)),
            pltpu.SemaphoreType.DMA,
            pltpu.SemaphoreType.DMA,
            pltpu.SemaphoreType.DMA,
            pltpu.SemaphoreType.DMA((EARLY // BATCH + 1,)),
            pltpu.SemaphoreType.DMA((GROUPS // 2,)),
            pltpu.SemaphoreType.DMA,
            pltpu.SemaphoreType.DMA((2,)),
            pltpu.SemaphoreType.REGULAR,
            pltpu.SemaphoreType.REGULAR,
            pltpu.SemaphoreType.REGULAR,
            pltpu.SemaphoreType.REGULAR,
            pltpu.SemaphoreType.REGULAR,
            pltpu.SemaphoreType.DMA,
            pltpu.SemaphoreType.DMA((GROUPS,)),
            pltpu.SemaphoreType.DMA((2, rows)),
            pltpu.SemaphoreType.DMA((2, rows)),
        ],
        compiler_params=pltpu.CompilerParams(
            collective_id=0, has_side_effects=True, vmem_limit_bytes=60 * 1024 * 1024
        ),
        name="rounds",
    )(arrangement, blocks, rotations)
    return pl.pallas_call(
        write_results,
        out_shape=out_shape,
        in_specs=[vmem, vmem],
        out_specs=(hbm, hbm),
        scratch_shapes=[pltpu.SemaphoreType.DMA((2,))],
        name="write_results",
    )(
        pltpu.with_memory_space_constraint(rotated, pltpu.VMEM),
        pltpu.with_memory_space_constraint(grams, pltpu.VMEM),
    )


def solution(mesh):
    placed = (P("snap", "row", None), P(), P(None, "snap", None, None))
    return jax.shard_map(
        body,
        mesh=mesh,
        in_specs=placed,
        out_specs=(P(None, "row", "snap"), P(None, "snap", "row", None)),
        check_vma=False,
    )
```

```python
import functools

import jax
import jax.numpy as jnp
from jax import lax
from jax.experimental import pallas as pl
from jax.experimental.pallas import tpu as pltpu
from jax.sharding import PartitionSpec as P

MESH = pl.DeviceIdType.MESH
BATCH = 4
EARLY = 8
HELPER = 6
GROUPS = 8


def split(value):
    high = value.astype(jnp.bfloat16)
    low = (value - high.astype(jnp.float32)).astype(jnp.bfloat16)
    return high, low


def dot(left, right):
    return jnp.dot(left, right, preferred_element_type=jnp.float32)


def dot_rows(left, right):
    return lax.dot_general(left, right, (((0,), (0,)), ((), ())), preferred_element_type=jnp.float32)


def kernel(
    sizes,
    order_hbm,
    x_hbm,
    rot_hbm,
    out_ref,
    gram_ref,
    order_ref,
    x_ref,
    rot_ref,
    rot_before,
    stage,
    over,
    landed,
    rot_landed,
    blocks,
    extra,
    helped,
    first,
    second,
    arrived,
    rot_high,
    rot_low,
    before_high,
    before_low,
    shares,
    share_in,
    load_sem,
    a2a_send,
    a2a_recv,
    extra_send,
    extra_recv,
    before_send,
    before_recv,
    over_send,
    over_recv,
    rot_send,
    rot_recv,
    help_send,
    partner_in,
    partners_in,
    half_in,
    rows_in,
    rows_all_in,
    next_send,
    next_recv,
    share_send,
    share_recv,
):
    snaps, rows, modes, delays, width = sizes
    half = width // 2
    per_group = snaps // GROUPS
    group_modes = modes * per_group
    group_rows = group_modes * delays
    share_rows = width // rows
    scale = 1.0 / float(modes * snaps * delays * rows)

    me = lax.axis_index("snap")
    row = lax.axis_index("row")
    my_group = me // per_group
    after = (me + 1) % snaps
    run = snaps // 2
    is_head = me % run == 0
    is_last = me % run == run - 1

    loads = [
        pltpu.make_async_copy(order_hbm, order_ref, load_sem.at[0]),
        pltpu.make_async_copy(x_hbm, x_ref, load_sem.at[1]),
        pltpu.make_async_copy(rot_hbm, rot_ref, load_sem.at[2]),
    ]
    for load in loads:
        load.start()

    barrier = pltpu.get_barrier_semaphore()
    high_part = me // run
    in_low, in_high = high_part == 0, high_part == 1
    my_head = high_part * run
    across = (me + run) % snaps
    my_span = pl.ds(me * modes, modes)
    across_span = pl.ds(across * modes, modes)
    across_group = across // per_group
    ys = GROUPS // 2
    my_y = my_group % ys
    my_place = me % per_group

    def signal(semaphore, snap, to_row):
        pl.semaphore_signal(
            semaphore, inc=1, device_id={"snap": snap, "row": to_row}, device_id_type=MESH
        )

    def remote(source, target, send, recv, snap):
        return pltpu.make_async_remote_copy(
            src_ref=source,
            dst_ref=target,
            send_sem=send,
            recv_sem=recv,
            device_id={"snap": snap, "row": row},
            device_id_type=MESH,
        )

    def place_at(i):
        k, j = i // per_group, i % per_group
        return ((my_y + k) % ys) * per_group + (my_place + j) % per_group

    def take(target, d):
        target[:, :, :half] = x_ref[:, order_ref[2 * d]]
        target[:, :, half:] = x_ref[:, order_ref[2 * d + 1]]

    def cross_copy(batch):
        span = pl.ds(batch * BATCH, BATCH)
        return remote(over.at[span], landed.at[span], over_send, over_recv.at[batch], across)

    def cross_extra():
        return remote(over.at[EARLY], landed.at[EARLY], over_send, over_recv.at[batches], across)

    def send_across():
        @pl.when(is_last)
        def _():
            rot_across.start()

        @pl.loop(0, batches)
        def _(batch):
            @pl.loop(0, BATCH)
            def _(j):
                i = batch * BATCH + j
                take(over.at[i], (run - my_head) + place_at(i))

            cross_copy(batch).start()

            @pl.when(batch == 1)
            def _():
                take(over.at[EARLY], (run - my_head + snaps - 1) % snaps)
                cross_extra().start()

    helper = my_head + my_y * per_group + HELPER
    is_helper = my_place == HELPER
    place_span = pl.ds(my_place * modes, modes)
    other_pair = (my_head + snaps - 1) % snaps

    def send_inside(i):
        d = my_head + place_at(i)
        take(stage.at[i], d)
        remote(stage.at[i], blocks.at[my_span], a2a_send, a2a_recv.at[my_group], d).start()

        @pl.when(d == helper)
        def _():
            take(stage.at[0], other_pair)
            remote(
                stage.at[0], extra.at[0, place_span], extra_send, extra_recv.at[0], helper
            ).start()

    def send_direct(i):
        d = run - my_head + place_at(i)
        take(stage.at[run + i], d)
        remote(stage.at[run + i], blocks.at[my_span], a2a_send, a2a_recv.at[my_group], d).start()

    batches = EARLY // BATCH
    rot_across = remote(
        rot_ref.at[0, 0, :, pl.ds(half, half)], rot_landed, before_send, rot_recv, across
    )
    rot_on = [
        remote(rot_landed, rot_before, rot_send.at[y], before_recv, my_head + y * per_group + HELPER)
        for y in range(ys)
    ]

    def prepare():
        take(blocks.at[my_span], me)

        @pl.when(is_helper)
        def _():
            take(extra.at[0, place_span], other_pair)

        for r in range(2):
            high, low = split(rot_ref[r, 0])
            rot_high[r] = high
            rot_low[r] = low
        shares[...] = jnp.zeros_like(shares)

    @pl.when(in_low)
    def _():
        signal(barrier, across, row)

        @pl.loop(1, run)
        def _(i):
            signal(barrier, (me + i) % run, row)

        for i in range(1, rows):
            signal(barrier, me, (row + i) % rows)

        for load in loads:
            load.wait()
        pl.semaphore_wait(barrier, run - 1 + rows - 1)
        signal(barrier, across, row)
        pl.semaphore_wait(partner_in, 1)

        @pl.loop(1, run)
        def _(i):
            signal(partners_in, (me + i) % run, row)

        send_across()

        @pl.loop(1, run)
        def _(i):
            send_inside(i)

        pl.semaphore_wait(partners_in, run - 1)
        signal(half_in, across, row)
        for i in range(1, rows):
            signal(rows_in, me, (row + i) % rows)

        @pl.loop(EARLY, run)
        def _(i):
            send_direct(i)

        prepare()
        pl.semaphore_wait(rows_in, rows - 1)
        signal(rows_all_in, across, row)

    @pl.when(in_high)
    def _():
        pl.semaphore_wait(barrier, 1)
        signal(partner_in, across, row)
        for load in loads:
            load.wait()
        send_across()
        pl.semaphore_wait(barrier, 1)

        @pl.loop(EARLY, run)
        def _(i):
            send_direct(i)

        prepare()
        pl.semaphore_wait(half_in, 1)

        @pl.loop(1, run)
        def _(i):
            send_inside(i)


    def pass_on(batch):
        cross_copy(batch).wait_recv()

        @pl.loop(0, BATCH)
        def _(j):
            i = batch * BATCH + j
            d = my_head + place_at(i)

            @pl.when(i == 0)
            def _():
                blocks[across_span] = landed[0]

            @pl.when(i > 0)
            def _():
                remote(
                    landed.at[i], blocks.at[across_span], a2a_send, a2a_recv.at[across_group], d
                ).start()

    def pass_extra_on():
        cross_extra().wait_recv()

        @pl.when(is_helper)
        def _():
            extra[1, place_span] = landed[EARLY]

        @pl.when(jnp.logical_not(is_helper))
        def _():
            remote(
                landed.at[EARLY], extra.at[1, place_span], extra_send, extra_recv.at[1], helper
            ).start()

    def help_first(side):
        group = (my_group, across_group)[side]
        part = extra.at[side, pl.ds(0, group_modes - modes)]
        pltpu.make_async_copy(part, part, extra_recv.at[side]).wait()
        high, low = split(extra[side].reshape(group_rows, width))
        other = dot(high, before_high[...]) + (
            dot(high, before_low[...]) + dot(low, before_high[...])
        )
        helped[side] = other.reshape(group_modes, delays, half)
        help_copy(side, group).start()

    def help_copy(side, group):
        span = pl.ds(group * group_modes, group_modes)
        return remote(
            helped.at[side], arrived.at[span], help_send.at[side], next_recv.at[group], my_head
        )

    def pass_on_all():
        @pl.when(is_last)
        def _():
            rot_across.wait_recv()
            for copy in rot_on:
                copy.start()

        for batch in range(batches):
            pass_on(batch)
        pass_extra_on()

    def wait_group(buffer, sems, group):
        whole = buffer.at[pl.ds(0, group_modes)]
        part = buffer.at[pl.ds(0, group_modes - modes)]

        @pl.when(group % ys == my_y)
        def _():
            pltpu.make_async_copy(part, part, sems.at[group]).wait()

        @pl.when(group % ys != my_y)
        def _():
            pltpu.make_async_copy(whole, whole, sems.at[group]).wait()

    def turn(r, matrix):
        high, low = split(matrix)
        return dot(high, rot_high[r]) + (dot(high, rot_low[r]) + dot(low, rot_high[r]))

    def add_gram(r, turned):
        high, low = split(turned)
        part = dot_rows(high, high) + (dot_rows(high, low) + dot_rows(low, high))
        shares[r] += part.reshape(rows, share_rows, width)

    def send_next(group):
        span = pl.ds(group * group_modes, group_modes)
        return pltpu.make_async_remote_copy(
            src_ref=second.at[span],
            dst_ref=arrived.at[span],
            send_sem=next_send,
            recv_sem=next_recv.at[group],
            device_id={"snap": after, "row": row},
            device_id_type=MESH,
        )

    def group_of(crossing, k):
        return (high_part + crossing) % 2 * ys + (my_y + ys - k % ys) % ys

    def in_order(i):
        crossing = jnp.where(jnp.logical_or(i == 2, i >= 5), 1, 0)
        before = jnp.where(i >= 5, i - 4, jnp.where(i == 2, 0, jnp.where(i > 2, i - 1, i)))
        return crossing, before

    def round_one(k):
        group = group_of(*in_order(k))
        span = pl.ds(group * group_modes, group_modes)
        wait_group(blocks, a2a_recv, group)
        turned = turn(0, blocks[span].reshape(group_rows, width))
        first[span] = turned[:, :half].reshape(group_modes, delays, half)
        second[span] = turned[:, half:].reshape(group_modes, delays, half)

        @pl.when(jnp.logical_not(is_last))
        def _():
            send_next(group).start()

        add_gram(0, turned)

    wraps = jnp.logical_and(my_place == 0, jnp.logical_not(is_head))

    def round_two(k):
        crossing, step = in_order(k)
        group = jnp.where(wraps, group_of(k // ys, k % ys + 1), group_of(crossing, step))
        group = jnp.where(is_head, group_of(k // ys, k % ys), group)
        span = pl.ds(group * group_modes, group_modes)

        send_next(group).wait_recv()
        matrix = jnp.concatenate([first[span], arrived[span]], axis=2)
        turned = turn(1, matrix.reshape(group_rows, width))
        out_ref[span] = turned.reshape(group_modes, delays, width)
        add_gram(1, turned)

    def finish(r):
        for i in range(1, rows):
            share_copy(r, i).start()

    def share_copy(r, i):
        to = (row + i) % rows
        return pltpu.make_async_remote_copy(
            src_ref=shares.at[r, to],
            dst_ref=share_in.at[r, i],
            send_sem=share_send.at[r, i],
            recv_sem=share_recv.at[r, i],
            device_id={"snap": me, "row": to},
            device_id_type=MESH,
        )

    def collect(r):
        for i in range(1, rows):
            share_copy(r, i).wait()
        total = shares[r, row]
        for i in range(1, rows):
            total = total + share_in[r, i]
        gram_ref[r, 0] = total * scale

    pass_on_all()

    @pl.loop(0, GROUPS)
    def _(k):
        round_one(k)

        @pl.when(jnp.logical_and(is_helper, k == 3))
        def _():
            rot_on[0].wait_recv()
            high, low = split(rot_before[...])
            before_high[...] = high
            before_low[...] = low
            help_first(0)

        @pl.when(jnp.logical_and(is_helper, k == 5))
        def _():
            help_first(1)

        @pl.loop(jnp.where(k == 6, 4, 0), jnp.where(k == 5, 4, jnp.where(k == 6, 6, 0)))
        def _(j):
            round_two(j)

    @pl.when(in_high)
    def _():
        pl.semaphore_wait(rows_all_in, 1)

    finish(0)

    @pl.loop(GROUPS - 2, GROUPS)
    def _(j):
        round_two(j)

    finish(1)
    collect(0)
    sent = blocks.at[pl.ds(0, 2 * (run - 1) * modes)]
    pltpu.make_async_copy(sent, sent, a2a_send).wait()
    pltpu.make_async_copy(over, over, over_send).wait()

    @pl.when(jnp.logical_not(is_helper))
    def _():
        two = stage.at[pl.ds(0, 2)]
        pltpu.make_async_copy(two, two, extra_send).wait()

    @pl.when(is_helper)
    def _():
        for side in range(2):
            help_copy(side, (my_group, across_group)[side]).wait_send()

    @pl.when(is_last)
    def _():
        rot_across.wait_send()
        for copy in rot_on:
            copy.wait_send()

    @pl.when(jnp.logical_not(is_last))
    def _():
        pltpu.make_async_copy(second, second, next_send).wait()

    collect(1)


def write_results(out_from, gram_from, out_ref, gram_ref, sems):
    copies = [
        pltpu.make_async_copy(out_from, out_ref, sems.at[0]),
        pltpu.make_async_copy(gram_from, gram_ref, sems.at[1]),
    ]
    for copy in copies:
        copy.start()
    for copy in copies:
        copy.wait()


def body(delay_matrix, arrangement, rotations):
    modes, delays, columns = delay_matrix.shape
    snaps = lax.axis_size("snap")
    rows = lax.axis_size("row")
    width = columns // snaps
    half = width // 2
    share_rows = width // rows
    sizes = (snaps, rows, modes, delays, width)
    f32, bf16 = jnp.float32, jnp.bfloat16
    blocks = delay_matrix.reshape(modes, delays, 2 * snaps, half).transpose(0, 2, 1, 3)
    hbm = pl.BlockSpec(memory_space=pltpu.HBM)
    vmem = pl.BlockSpec(memory_space=pltpu.VMEM)
    out_shape = (
        jax.ShapeDtypeStruct((snaps * modes, delays, width), f32),
        jax.ShapeDtypeStruct((2, 1, share_rows, width), f32),
    )
    rotated, grams = pl.pallas_call(
        functools.partial(kernel, sizes),
        out_shape=tuple(pltpu.VMEM(s.shape, s.dtype) for s in out_shape),
        in_specs=[hbm, hbm, hbm],
        out_specs=(vmem, vmem),
        scratch_shapes=[
            pltpu.SMEM(arrangement.shape, arrangement.dtype),
            pltpu.VMEM(blocks.shape, f32),
            pltpu.VMEM(rotations.shape, f32),
            pltpu.VMEM((width, half), f32),
            pltpu.VMEM((snaps, modes, delays, width), f32),
            pltpu.VMEM((EARLY + 1, modes, delays, width), f32),
            pltpu.VMEM((EARLY + 1, modes, delays, width), f32),
            pltpu.VMEM((width, half), f32),
            pltpu.VMEM((snaps * modes, delays, width), f32),
            pltpu.VMEM((2, snaps // GROUPS * modes, delays, width), f32),
            pltpu.VMEM((2, snaps // GROUPS * modes, delays, half), f32),
            pltpu.VMEM((snaps * modes, delays, half), f32),
            pltpu.VMEM((snaps * modes, delays, half), f32),
            pltpu.VMEM((snaps * modes, delays, half), f32),
            pltpu.VMEM((2, width, width), bf16),
            pltpu.VMEM((2, width, width), bf16),
            pltpu.VMEM((width, half), bf16),
            pltpu.VMEM((width, half), bf16),
            pltpu.VMEM((2, rows, share_rows, width), f32),
            pltpu.VMEM((2, rows, share_rows, width), f32),
            pltpu.SemaphoreType.DMA((3,)),
            pltpu.SemaphoreType.DMA,
            pltpu.SemaphoreType.DMA((GROUPS,)),
            pltpu.SemaphoreType.DMA,
            pltpu.SemaphoreType.DMA((2,)),
            pltpu.SemaphoreType.DMA,
            pltpu.SemaphoreType.DMA,
            pltpu.SemaphoreType.DMA,
            pltpu.SemaphoreType.DMA((EARLY // BATCH + 1,)),
            pltpu.SemaphoreType.DMA((GROUPS // 2,)),
            pltpu.SemaphoreType.DMA,
            pltpu.SemaphoreType.DMA((2,)),
            pltpu.SemaphoreType.REGULAR,
            pltpu.SemaphoreType.REGULAR,
            pltpu.SemaphoreType.REGULAR,
            pltpu.SemaphoreType.REGULAR,
            pltpu.SemaphoreType.REGULAR,
            pltpu.SemaphoreType.DMA,
            pltpu.SemaphoreType.DMA((GROUPS,)),
            pltpu.SemaphoreType.DMA((2, rows)),
            pltpu.SemaphoreType.DMA((2, rows)),
        ],
        compiler_params=pltpu.CompilerParams(
            collective_id=0, has_side_effects=True, vmem_limit_bytes=60 * 1024 * 1024
        ),
        name="rounds",
    )(arrangement, blocks, rotations)
    return pl.pallas_call(
        write_results,
        out_shape=out_shape,
        in_specs=[vmem, vmem],
        out_specs=(hbm, hbm),
        scratch_shapes=[pltpu.SemaphoreType.DMA((2,))],
        name="write_results",
    )(
        pltpu.with_memory_space_constraint(rotated, pltpu.VMEM),
        pltpu.with_memory_space_constraint(grams, pltpu.VMEM),
    )


def solution(mesh):
    placed = (P("snap", "row", None), P(), P(None, "snap", None, None))
    return jax.shard_map(
        body,
        mesh=mesh,
        in_specs=placed,
        out_specs=(P(None, "row", "snap"), P(None, "snap", "row", None)),
        check_vma=False,
    )
```

```python
import functools

import jax
import jax.numpy as jnp
from jax import lax
from jax.experimental import pallas as pl
from jax.experimental.pallas import tpu as pltpu
from jax.sharding import PartitionSpec as P

MESH = pl.DeviceIdType.MESH
BATCH = 4
EARLY = 8
HELPER = 6
GROUPS = 8


def split(value):
    high = value.astype(jnp.bfloat16)
    low = (value - high.astype(jnp.float32)).astype(jnp.bfloat16)
    return high, low


def dot(left, right):
    return jnp.dot(left, right, preferred_element_type=jnp.float32)


def dot_rows(left, right):
    return lax.dot_general(left, right, (((0,), (0,)), ((), ())), preferred_element_type=jnp.float32)


def kernel(
    sizes,
    order_hbm,
    x_hbm,
    rot_hbm,
    out_ref,
    gram_ref,
    order_ref,
    x_ref,
    rot_ref,
    rot_before,
    stage,
    over,
    landed,
    rot_landed,
    blocks,
    extra,
    helped,
    first,
    second,
    arrived,
    rot_high,
    rot_low,
    before_high,
    before_low,
    shares,
    share_in,
    merge_in,
    load_sem,
    a2a_send,
    a2a_recv,
    extra_send,
    extra_recv,
    before_send,
    before_recv,
    over_send,
    over_recv,
    rot_send,
    rot_recv,
    help_send,
    partner_in,
    partners_in,
    half_in,
    rows_in,
    rows_all_in,
    next_send,
    next_recv,
    share_send,
    share_recv,
    merge_send,
    merge_recv,
):
    snaps, rows, modes, delays, width = sizes
    half = width // 2
    per_group = snaps // GROUPS
    group_modes = modes * per_group
    group_rows = group_modes * delays
    share_rows = width // rows
    scale = 1.0 / float(modes * snaps * delays * rows)

    me = lax.axis_index("snap")
    row = lax.axis_index("row")
    my_group = me // per_group
    after = (me + 1) % snaps
    run = snaps // 2
    is_head = me % run == 0
    is_last = me % run == run - 1

    loads = [
        pltpu.make_async_copy(order_hbm, order_ref, load_sem.at[0]),
        pltpu.make_async_copy(x_hbm, x_ref, load_sem.at[1]),
        pltpu.make_async_copy(rot_hbm, rot_ref, load_sem.at[2]),
    ]
    for load in loads:
        load.start()

    barrier = pltpu.get_barrier_semaphore()
    high_part = me // run
    in_low, in_high = high_part == 0, high_part == 1
    my_head = high_part * run
    across = (me + run) % snaps
    my_span = pl.ds(me * modes, modes)
    across_span = pl.ds(across * modes, modes)
    across_group = across // per_group
    ys = GROUPS // 2
    my_y = my_group % ys
    my_place = me % per_group

    def signal(semaphore, snap, to_row):
        pl.semaphore_signal(
            semaphore, inc=1, device_id={"snap": snap, "row": to_row}, device_id_type=MESH
        )

    def remote(source, target, send, recv, snap):
        return pltpu.make_async_remote_copy(
            src_ref=source,
            dst_ref=target,
            send_sem=send,
            recv_sem=recv,
            device_id={"snap": snap, "row": row},
            device_id_type=MESH,
        )

    def place_at(i):
        k, j = i // per_group, i % per_group
        return ((my_y + k) % ys) * per_group + (my_place + j) % per_group

    def take(target, d):
        target[:, :, :half] = x_ref[:, order_ref[2 * d]]
        target[:, :, half:] = x_ref[:, order_ref[2 * d + 1]]

    def cross_copy(batch):
        span = pl.ds(batch * BATCH, BATCH)
        return remote(over.at[span], landed.at[span], over_send, over_recv.at[batch], across)

    def cross_extra():
        return remote(over.at[EARLY], landed.at[EARLY], over_send, over_recv.at[batches], across)

    def send_across():
        @pl.when(is_last)
        def _():
            rot_across.start()

        @pl.loop(0, batches)
        def _(batch):
            @pl.loop(0, BATCH)
            def _(j):
                i = batch * BATCH + j
                take(over.at[i], (run - my_head) + place_at(i))

            cross_copy(batch).start()

            @pl.when(batch == 1)
            def _():
                take(over.at[EARLY], (run - my_head + snaps - 1) % snaps)
                cross_extra().start()

    helper = my_head + my_y * per_group + HELPER
    is_helper = my_place == HELPER
    place_span = pl.ds(my_place * modes, modes)
    other_pair = (my_head + snaps - 1) % snaps

    def send_inside(i):
        d = my_head + place_at(i)
        take(stage.at[i], d)
        remote(stage.at[i], blocks.at[my_span], a2a_send, a2a_recv.at[my_group], d).start()

        @pl.when(d == helper)
        def _():
            take(stage.at[0], other_pair)
            remote(
                stage.at[0], extra.at[0, place_span], extra_send, extra_recv.at[0], helper
            ).start()

    def send_direct(i):
        d = run - my_head + place_at(i)
        take(stage.at[run + i], d)
        remote(stage.at[run + i], blocks.at[my_span], a2a_send, a2a_recv.at[my_group], d).start()

    batches = EARLY // BATCH
    rot_across = remote(
        rot_ref.at[0, 0, :, pl.ds(half, half)], rot_landed, before_send, rot_recv, across
    )
    rot_on = [
        remote(rot_landed, rot_before, rot_send.at[y], before_recv, my_head + y * per_group + HELPER)
        for y in range(ys)
    ]

    def prepare():
        take(blocks.at[my_span], me)

        @pl.when(is_helper)
        def _():
            take(extra.at[0, place_span], other_pair)

        for r in range(2):
            high, low = split(rot_ref[r, 0])
            rot_high[r] = high
            rot_low[r] = low
        shares[...] = jnp.zeros_like(shares)

    @pl.when(in_low)
    def _():
        signal(barrier, across, row)

        @pl.loop(1, run)
        def _(i):
            signal(barrier, (me + i) % run, row)

        for i in range(1, rows):
            signal(barrier, me, (row + i) % rows)

        for load in loads:
            load.wait()
        pl.semaphore_wait(barrier, run - 1 + rows - 1)
        signal(barrier, across, row)
        pl.semaphore_wait(partner_in, 1)

        @pl.loop(1, run)
        def _(i):
            signal(partners_in, (me + i) % run, row)

        send_across()

        @pl.loop(1, run)
        def _(i):
            send_inside(i)

        pl.semaphore_wait(partners_in, run - 1)
        signal(half_in, across, row)
        for i in range(1, rows):
            signal(rows_in, me, (row + i) % rows)

        @pl.loop(EARLY, run)
        def _(i):
            send_direct(i)

        prepare()
        pl.semaphore_wait(rows_in, rows - 1)
        signal(rows_all_in, across, row)

    @pl.when(in_high)
    def _():
        pl.semaphore_wait(barrier, 1)
        signal(partner_in, across, row)
        for load in loads:
            load.wait()
        send_across()
        pl.semaphore_wait(barrier, 1)

        @pl.loop(EARLY, run)
        def _(i):
            send_direct(i)

        prepare()
        pl.semaphore_wait(half_in, 1)

        @pl.loop(1, run)
        def _(i):
            send_inside(i)


    def pass_on(batch):
        cross_copy(batch).wait_recv()

        @pl.loop(0, BATCH)
        def _(j):
            i = batch * BATCH + j
            d = my_head + place_at(i)

            @pl.when(i == 0)
            def _():
                blocks[across_span] = landed[0]

            @pl.when(i > 0)
            def _():
                remote(
                    landed.at[i], blocks.at[across_span], a2a_send, a2a_recv.at[across_group], d
                ).start()

    def pass_extra_on():
        cross_extra().wait_recv()

        @pl.when(is_helper)
        def _():
            extra[1, place_span] = landed[EARLY]

        @pl.when(jnp.logical_not(is_helper))
        def _():
            remote(
                landed.at[EARLY], extra.at[1, place_span], extra_send, extra_recv.at[1], helper
            ).start()

    def help_first(side):
        group = (my_group, across_group)[side]
        part = extra.at[side, pl.ds(0, group_modes - modes)]
        pltpu.make_async_copy(part, part, extra_recv.at[side]).wait()
        high, low = split(extra[side].reshape(group_rows, width))
        other = dot(high, before_high[...]) + (
            dot(high, before_low[...]) + dot(low, before_high[...])
        )
        helped[side] = other.reshape(group_modes, delays, half)
        help_copy(side, group).start()

    def help_copy(side, group):
        span = pl.ds(group * group_modes, group_modes)
        return remote(
            helped.at[side], arrived.at[span], help_send.at[side], next_recv.at[group], my_head
        )

    def pass_on_all():
        @pl.when(is_last)
        def _():
            rot_across.wait_recv()
            for copy in rot_on:
                copy.start()

        for batch in range(batches):
            pass_on(batch)
        pass_extra_on()

    def wait_group(buffer, sems, group):
        whole = buffer.at[pl.ds(0, group_modes)]
        part = buffer.at[pl.ds(0, group_modes - modes)]

        @pl.when(group % ys == my_y)
        def _():
            pltpu.make_async_copy(part, part, sems.at[group]).wait()

        @pl.when(group % ys != my_y)
        def _():
            pltpu.make_async_copy(whole, whole, sems.at[group]).wait()

    def turn(r, matrix):
        high, low = split(matrix)
        return dot(high, rot_high[r]) + (dot(high, rot_low[r]) + dot(low, rot_high[r]))

    def add_gram(r, turned):
        high, low = split(turned)
        part = dot_rows(high, high) + (dot_rows(high, low) + dot_rows(low, high))
        shares[r] += part.reshape(rows, share_rows, width)

    def send_next(group):
        span = pl.ds(group * group_modes, group_modes)
        return pltpu.make_async_remote_copy(
            src_ref=second.at[span],
            dst_ref=arrived.at[span],
            send_sem=next_send,
            recv_sem=next_recv.at[group],
            device_id={"snap": after, "row": row},
            device_id_type=MESH,
        )

    def group_of(crossing, k):
        return (high_part + crossing) % 2 * ys + (my_y + ys - k % ys) % ys

    def in_order(i):
        crossing = jnp.where(jnp.logical_or(i == 2, i >= 5), 1, 0)
        before = jnp.where(i >= 5, i - 4, jnp.where(i == 2, 0, jnp.where(i > 2, i - 1, i)))
        return crossing, before

    def round_one(k):
        group = group_of(*in_order(k))
        span = pl.ds(group * group_modes, group_modes)
        wait_group(blocks, a2a_recv, group)
        turned = turn(0, blocks[span].reshape(group_rows, width))
        first[span] = turned[:, :half].reshape(group_modes, delays, half)
        second[span] = turned[:, half:].reshape(group_modes, delays, half)

        @pl.when(jnp.logical_not(is_last))
        def _():
            send_next(group).start()

        add_gram(0, turned)

    wraps = jnp.logical_and(my_place == 0, jnp.logical_not(is_head))

    def round_two(k):
        crossing, step = in_order(k)
        group = jnp.where(wraps, group_of(k // ys, k % ys + 1), group_of(crossing, step))
        group = jnp.where(is_head, group_of(k // ys, k % ys), group)
        span = pl.ds(group * group_modes, group_modes)

        send_next(group).wait_recv()
        matrix = jnp.concatenate([first[span], arrived[span]], axis=2)
        turned = turn(1, matrix.reshape(group_rows, width))
        out_ref[span] = turned.reshape(group_modes, delays, width)
        add_gram(1, turned)

    inner = jnp.logical_or(row == 1, row == 2)
    outer = jnp.logical_not(inner)
    near = row + 1 - 2 * (row % 2)

    def row_copy(source, target, send, recv, to):
        return pltpu.make_async_remote_copy(
            src_ref=source,
            dst_ref=target,
            send_sem=send,
            recv_sem=recv,
            device_id={"snap": me, "row": to},
            device_id_type=MESH,
        )

    def share_copy(r, i):
        to = (row + i) % rows
        return row_copy(
            shares.at[r, to], share_in.at[r, i], share_send.at[r, i], share_recv.at[r, i], to
        )

    def merge_copy(r):
        return row_copy(
            shares.at[r, rows - 1 - row], merge_in.at[r], merge_send.at[r], merge_recv.at[r], near
        )

    def skips(i):
        return jnp.logical_and(outer, (row + i) % rows == rows - 1 - row)

    def finish(r):
        @pl.when(outer)
        def _():
            merge_copy(r).start()

        for i in range(1, rows):

            @pl.when(jnp.logical_not(jnp.logical_or(skips(i), jnp.logical_and(inner, i == 2))))
            def _():
                share_copy(r, i).start()

    def forward(r):
        @pl.when(inner)
        def _():
            merge_copy(r).wait_recv()
            far = (row + 2) % rows
            shares[r, far] = shares[r, far] + merge_in[r]
            share_copy(r, 2).start()

    def collect(r):
        total = shares[r, row]
        gram_ref[r, 0] = total

        for i in range(1, rows):
            from_far = jnp.logical_and(outer, (row + rows - i) % rows == rows - 1 - row)

            @pl.when(jnp.logical_not(from_far))
            def _():
                share_copy(r, i).wait_recv()
                gram_ref[r, 0] += share_in[r, i]

            @pl.when(jnp.logical_not(skips(i)))
            def _():
                share_copy(r, i).wait_send()

        gram_ref[r, 0] = gram_ref[r, 0] * scale

        @pl.when(outer)
        def _():
            merge_copy(r).wait_send()

    pass_on_all()

    @pl.loop(0, GROUPS)
    def _(k):
        round_one(k)

        @pl.when(jnp.logical_and(is_helper, k == 3))
        def _():
            rot_on[0].wait_recv()
            high, low = split(rot_before[...])
            before_high[...] = high
            before_low[...] = low
            help_first(0)

        @pl.when(jnp.logical_and(is_helper, k == 5))
        def _():
            help_first(1)

        early = jnp.where(is_head, 0, 4)

        @pl.loop(jnp.where(k == 6, early, 0), jnp.where(k == 5, early, jnp.where(k == 6, 6, 0)))
        def _(j):
            round_two(j)

    @pl.when(in_high)
    def _():
        pl.semaphore_wait(rows_all_in, 1)

    finish(0)

    @pl.loop(GROUPS - 2, GROUPS)
    def _(j):
        round_two(j)

    forward(0)

    @pl.when(row == 2)
    def _():
        forward(1)

    finish(1)

    @pl.when(row == 1)
    def _():
        forward(1)

    collect(0)
    sent = blocks.at[pl.ds(0, 2 * (run - 1) * modes)]
    pltpu.make_async_copy(sent, sent, a2a_send).wait()
    pltpu.make_async_copy(over, over, over_send).wait()

    @pl.when(jnp.logical_not(is_helper))
    def _():
        two = stage.at[pl.ds(0, 2)]
        pltpu.make_async_copy(two, two, extra_send).wait()

    @pl.when(is_helper)
    def _():
        for side in range(2):
            help_copy(side, (my_group, across_group)[side]).wait_send()

    @pl.when(is_last)
    def _():
        rot_across.wait_send()
        for copy in rot_on:
            copy.wait_send()

    @pl.when(jnp.logical_not(is_last))
    def _():
        pltpu.make_async_copy(second, second, next_send).wait()

    collect(1)


def write_results(out_from, gram_from, out_ref, gram_ref, sems):
    copies = [
        pltpu.make_async_copy(out_from, out_ref, sems.at[0]),
        pltpu.make_async_copy(gram_from, gram_ref, sems.at[1]),
    ]
    for copy in copies:
        copy.start()
    for copy in copies:
        copy.wait()


def body(delay_matrix, arrangement, rotations):
    modes, delays, columns = delay_matrix.shape
    snaps = lax.axis_size("snap")
    rows = lax.axis_size("row")
    width = columns // snaps
    half = width // 2
    share_rows = width // rows
    sizes = (snaps, rows, modes, delays, width)
    f32, bf16 = jnp.float32, jnp.bfloat16
    blocks = delay_matrix.reshape(modes, delays, 2 * snaps, half).transpose(0, 2, 1, 3)
    hbm = pl.BlockSpec(memory_space=pltpu.HBM)
    vmem = pl.BlockSpec(memory_space=pltpu.VMEM)
    out_shape = (
        jax.ShapeDtypeStruct((snaps * modes, delays, width), f32),
        jax.ShapeDtypeStruct((2, 1, share_rows, width), f32),
    )
    rotated, grams = pl.pallas_call(
        functools.partial(kernel, sizes),
        out_shape=tuple(pltpu.VMEM(s.shape, s.dtype) for s in out_shape),
        in_specs=[hbm, hbm, hbm],
        out_specs=(vmem, vmem),
        scratch_shapes=[
            pltpu.SMEM(arrangement.shape, arrangement.dtype),
            pltpu.VMEM(blocks.shape, f32),
            pltpu.VMEM(rotations.shape, f32),
            pltpu.VMEM((width, half), f32),
            pltpu.VMEM((snaps, modes, delays, width), f32),
            pltpu.VMEM((EARLY + 1, modes, delays, width), f32),
            pltpu.VMEM((EARLY + 1, modes, delays, width), f32),
            pltpu.VMEM((width, half), f32),
            pltpu.VMEM((snaps * modes, delays, width), f32),
            pltpu.VMEM((2, snaps // GROUPS * modes, delays, width), f32),
            pltpu.VMEM((2, snaps // GROUPS * modes, delays, half), f32),
            pltpu.VMEM((snaps * modes, delays, half), f32),
            pltpu.VMEM((snaps * modes, delays, half), f32),
            pltpu.VMEM((snaps * modes, delays, half), f32),
            pltpu.VMEM((2, width, width), bf16),
            pltpu.VMEM((2, width, width), bf16),
            pltpu.VMEM((width, half), bf16),
            pltpu.VMEM((width, half), bf16),
            pltpu.VMEM((2, rows, share_rows, width), f32),
            pltpu.VMEM((2, rows, share_rows, width), f32),
            pltpu.VMEM((2, share_rows, width), f32),
            pltpu.SemaphoreType.DMA((3,)),
            pltpu.SemaphoreType.DMA,
            pltpu.SemaphoreType.DMA((GROUPS,)),
            pltpu.SemaphoreType.DMA,
            pltpu.SemaphoreType.DMA((2,)),
            pltpu.SemaphoreType.DMA,
            pltpu.SemaphoreType.DMA,
            pltpu.SemaphoreType.DMA,
            pltpu.SemaphoreType.DMA((EARLY // BATCH + 1,)),
            pltpu.SemaphoreType.DMA((GROUPS // 2,)),
            pltpu.SemaphoreType.DMA,
            pltpu.SemaphoreType.DMA((2,)),
            pltpu.SemaphoreType.REGULAR,
            pltpu.SemaphoreType.REGULAR,
            pltpu.SemaphoreType.REGULAR,
            pltpu.SemaphoreType.REGULAR,
            pltpu.SemaphoreType.REGULAR,
            pltpu.SemaphoreType.DMA,
            pltpu.SemaphoreType.DMA((GROUPS,)),
            pltpu.SemaphoreType.DMA((2, rows)),
            pltpu.SemaphoreType.DMA((2, rows)),
            pltpu.SemaphoreType.DMA((2,)),
            pltpu.SemaphoreType.DMA((2,)),
        ],
        compiler_params=pltpu.CompilerParams(
            collective_id=0, has_side_effects=True, vmem_limit_bytes=60 * 1024 * 1024
        ),
        name="rounds",
    )(arrangement, blocks, rotations)
    return pl.pallas_call(
        write_results,
        out_shape=out_shape,
        in_specs=[vmem, vmem],
        out_specs=(hbm, hbm),
        scratch_shapes=[pltpu.SemaphoreType.DMA((2,))],
        name="write_results",
    )(
        pltpu.with_memory_space_constraint(rotated, pltpu.VMEM),
        pltpu.with_memory_space_constraint(grams, pltpu.VMEM),
    )


def solution(mesh):
    placed = (P("snap", "row", None), P(), P(None, "snap", None, None))
    return jax.shard_map(
        body,
        mesh=mesh,
        in_specs=placed,
        out_specs=(P(None, "row", "snap"), P(None, "snap", "row", None)),
        check_vma=False,
    )
```

```python
import functools

import jax
import jax.numpy as jnp
from jax import lax
from jax.experimental import pallas as pl
from jax.experimental.pallas import tpu as pltpu
from jax.sharding import PartitionSpec as P

MESH = pl.DeviceIdType.MESH
BATCH = 4
EARLY = 8
HELPER = 6
GROUPS = 8


def split(value):
    high = value.astype(jnp.bfloat16)
    low = (value - high.astype(jnp.float32)).astype(jnp.bfloat16)
    return high, low


def dot(left, right):
    return jnp.dot(left, right, preferred_element_type=jnp.float32)


def dot_rows(left, right):
    return lax.dot_general(left, right, (((0,), (0,)), ((), ())), preferred_element_type=jnp.float32)


def kernel(
    sizes,
    order_hbm,
    x_hbm,
    rot_hbm,
    out_ref,
    gram_ref,
    order_ref,
    x_ref,
    rot_ref,
    rot_before,
    stage,
    over,
    landed,
    rot_landed,
    blocks,
    extra,
    helped,
    first,
    second,
    arrived,
    rot_high,
    rot_low,
    before_high,
    before_low,
    shares,
    share_in,
    merge_in,
    load_sem,
    a2a_send,
    a2a_recv,
    extra_send,
    extra_recv,
    before_send,
    before_recv,
    over_send,
    over_recv,
    rot_send,
    rot_recv,
    help_send,
    partner_in,
    partners_in,
    half_in,
    rows_in,
    rows_all_in,
    next_send,
    next_recv,
    share_send,
    share_recv,
    merge_send,
    merge_recv,
):
    snaps, rows, modes, delays, width = sizes
    half = width // 2
    per_group = snaps // GROUPS
    group_modes = modes * per_group
    group_rows = group_modes * delays
    share_rows = width // rows
    scale = 1.0 / float(modes * snaps * delays * rows)

    me = lax.axis_index("snap")
    row = lax.axis_index("row")
    my_group = me // per_group
    after = (me + 1) % snaps
    run = snaps // 2
    is_head = me % run == 0
    is_last = me % run == run - 1

    loads = [
        pltpu.make_async_copy(order_hbm, order_ref, load_sem.at[0]),
        pltpu.make_async_copy(x_hbm, x_ref, load_sem.at[1]),
        pltpu.make_async_copy(rot_hbm, rot_ref, load_sem.at[2]),
    ]
    for load in loads:
        load.start()

    barrier = pltpu.get_barrier_semaphore()
    high_part = me // run
    in_low, in_high = high_part == 0, high_part == 1
    my_head = high_part * run
    across = (me + run) % snaps
    my_span = pl.ds(me * modes, modes)
    across_span = pl.ds(across * modes, modes)
    across_group = across // per_group
    ys = GROUPS // 2
    my_y = my_group % ys
    my_place = me % per_group

    def signal(semaphore, snap, to_row):
        pl.semaphore_signal(
            semaphore, inc=1, device_id={"snap": snap, "row": to_row}, device_id_type=MESH
        )

    def remote(source, target, send, recv, snap):
        return pltpu.make_async_remote_copy(
            src_ref=source,
            dst_ref=target,
            send_sem=send,
            recv_sem=recv,
            device_id={"snap": snap, "row": row},
            device_id_type=MESH,
        )

    def place_at(i):
        k, j = i // per_group, i % per_group
        return ((my_y + k) % ys) * per_group + (my_place + j) % per_group

    def take(target, d):
        target[:, :, :half] = x_ref[:, order_ref[2 * d]]
        target[:, :, half:] = x_ref[:, order_ref[2 * d + 1]]

    def cross_copy(batch):
        span = pl.ds(batch * BATCH, BATCH)
        return remote(over.at[span], landed.at[span], over_send, over_recv.at[batch], across)

    def cross_extra():
        return remote(over.at[EARLY], landed.at[EARLY], over_send, over_recv.at[batches], across)

    def send_across():
        @pl.when(is_last)
        def _():
            rot_across.start()

        @pl.loop(0, batches)
        def _(batch):
            @pl.loop(0, BATCH)
            def _(j):
                i = batch * BATCH + j
                take(over.at[i], (run - my_head) + place_at(i))

            cross_copy(batch).start()

            @pl.when(batch == 1)
            def _():
                take(over.at[EARLY], (run - my_head + snaps - 1) % snaps)
                cross_extra().start()

    helper = my_head + my_y * per_group + HELPER
    is_helper = my_place == HELPER
    place_span = pl.ds(my_place * modes, modes)
    other_pair = (my_head + snaps - 1) % snaps

    def send_inside(i):
        d = my_head + place_at(i)
        take(stage.at[i], d)
        remote(stage.at[i], blocks.at[my_span], a2a_send, a2a_recv.at[my_group], d).start()

        @pl.when(d == helper)
        def _():
            take(stage.at[0], other_pair)
            remote(
                stage.at[0], extra.at[0, place_span], extra_send, extra_recv.at[0], helper
            ).start()

    def send_direct(i):
        d = run - my_head + place_at(i)
        take(stage.at[run + i], d)
        remote(stage.at[run + i], blocks.at[my_span], a2a_send, a2a_recv.at[my_group], d).start()

    batches = EARLY // BATCH
    rot_across = remote(
        rot_ref.at[0, 0, :, pl.ds(half, half)], rot_landed, before_send, rot_recv, across
    )
    rot_on = [
        remote(rot_landed, rot_before, rot_send.at[y], before_recv, my_head + y * per_group + HELPER)
        for y in range(ys)
    ]

    def prepare():
        take(blocks.at[my_span], me)

        @pl.when(is_helper)
        def _():
            take(extra.at[0, place_span], other_pair)

        for r in range(2):
            high, low = split(rot_ref[r, 0])
            rot_high[r] = high
            rot_low[r] = low
        shares[...] = jnp.zeros_like(shares)

    @pl.when(in_low)
    def _():
        signal(barrier, across, row)

        @pl.loop(1, run)
        def _(i):
            signal(barrier, (me + i) % run, row)

        for i in range(1, rows):
            signal(barrier, me, (row + i) % rows)

        for load in loads:
            load.wait()
        pl.semaphore_wait(barrier, run - 1 + rows - 1)
        signal(barrier, across, row)
        pl.semaphore_wait(partner_in, 1)

        @pl.loop(1, run)
        def _(i):
            signal(partners_in, (me + i) % run, row)

        send_across()

        @pl.loop(1, run)
        def _(i):
            send_inside(i)

        pl.semaphore_wait(partners_in, run - 1)
        signal(half_in, across, row)
        for i in range(1, rows):
            signal(rows_in, me, (row + i) % rows)

        @pl.loop(EARLY, run)
        def _(i):
            send_direct(i)

        prepare()
        pl.semaphore_wait(rows_in, rows - 1)
        signal(rows_all_in, across, row)

    @pl.when(in_high)
    def _():
        pl.semaphore_wait(barrier, 1)
        signal(partner_in, across, row)
        for load in loads:
            load.wait()
        send_across()
        pl.semaphore_wait(barrier, 1)

        @pl.loop(EARLY, run)
        def _(i):
            send_direct(i)

        prepare()
        pl.semaphore_wait(half_in, 1)

        @pl.loop(1, run)
        def _(i):
            send_inside(i)


    def pass_on(batch):
        cross_copy(batch).wait_recv()

        @pl.loop(0, BATCH)
        def _(j):
            i = batch * BATCH + j
            d = my_head + place_at(i)

            @pl.when(i == 0)
            def _():
                blocks[across_span] = landed[0]

            @pl.when(i > 0)
            def _():
                remote(
                    landed.at[i], blocks.at[across_span], a2a_send, a2a_recv.at[across_group], d
                ).start()

    def pass_extra_on():
        cross_extra().wait_recv()

        @pl.when(is_helper)
        def _():
            extra[1, place_span] = landed[EARLY]

        @pl.when(jnp.logical_not(is_helper))
        def _():
            remote(
                landed.at[EARLY], extra.at[1, place_span], extra_send, extra_recv.at[1], helper
            ).start()

    def help_first(side):
        group = (my_group, across_group)[side]
        part = extra.at[side, pl.ds(0, group_modes - modes)]
        pltpu.make_async_copy(part, part, extra_recv.at[side]).wait()
        high, low = split(extra[side].reshape(group_rows, width))
        other = dot(high, before_high[...]) + (
            dot(high, before_low[...]) + dot(low, before_high[...])
        )
        helped[side] = other.reshape(group_modes, delays, half)
        help_copy(side, group).start()

    def help_copy(side, group):
        span = pl.ds(group * group_modes, group_modes)
        return remote(
            helped.at[side], arrived.at[span], help_send.at[side], next_recv.at[group], my_head
        )

    def pass_on_all():
        @pl.when(is_last)
        def _():
            rot_across.wait_recv()
            for copy in rot_on:
                copy.start()

        for batch in range(batches):
            pass_on(batch)
        pass_extra_on()

    def wait_group(buffer, sems, group):
        whole = buffer.at[pl.ds(0, group_modes)]
        part = buffer.at[pl.ds(0, group_modes - modes)]

        @pl.when(group % ys == my_y)
        def _():
            pltpu.make_async_copy(part, part, sems.at[group]).wait()

        @pl.when(group % ys != my_y)
        def _():
            pltpu.make_async_copy(whole, whole, sems.at[group]).wait()

    def turn(r, matrix):
        high, low = split(matrix)
        return dot(high, rot_high[r]) + (dot(high, rot_low[r]) + dot(low, rot_high[r]))

    def add_gram(r, turned):
        high, low = split(turned)
        part = dot_rows(high, high) + (dot_rows(high, low) + dot_rows(low, high))
        shares[r] += part.reshape(rows, share_rows, width)

    def send_next(group):
        span = pl.ds(group * group_modes, group_modes)
        return pltpu.make_async_remote_copy(
            src_ref=second.at[span],
            dst_ref=arrived.at[span],
            send_sem=next_send,
            recv_sem=next_recv.at[group],
            device_id={"snap": after, "row": row},
            device_id_type=MESH,
        )

    def group_of(crossing, k):
        return (high_part + crossing) % 2 * ys + (my_y + ys - k % ys) % ys

    def in_order(i):
        crossing = jnp.where(jnp.logical_or(i == 2, i >= 5), 1, 0)
        before = jnp.where(i >= 5, i - 4, jnp.where(i == 2, 0, jnp.where(i > 2, i - 1, i)))
        return crossing, before

    def round_one(k):
        group = group_of(*in_order(k))
        span = pl.ds(group * group_modes, group_modes)
        wait_group(blocks, a2a_recv, group)
        turned = turn(0, blocks[span].reshape(group_rows, width))
        first[span] = turned[:, :half].reshape(group_modes, delays, half)
        second[span] = turned[:, half:].reshape(group_modes, delays, half)

        @pl.when(jnp.logical_not(is_last))
        def _():
            send_next(group).start()

        add_gram(0, turned)

    wraps = jnp.logical_and(my_place == 0, jnp.logical_not(is_head))

    def round_two(k):
        crossing, step = in_order(k)
        group = jnp.where(wraps, group_of(k // ys, k % ys + 1), group_of(crossing, step))
        group = jnp.where(is_head, group_of(k // ys, k % ys), group)
        span = pl.ds(group * group_modes, group_modes)

        send_next(group).wait_recv()
        matrix = jnp.concatenate([first[span], arrived[span]], axis=2)
        turned = turn(1, matrix.reshape(group_rows, width))
        out_ref[span] = turned.reshape(group_modes, delays, width)
        add_gram(1, turned)

    inner = jnp.logical_or(row == 1, row == 2)
    outer = jnp.logical_not(inner)
    near = row + 1 - 2 * (row % 2)

    def row_copy(source, target, send, recv, to):
        return pltpu.make_async_remote_copy(
            src_ref=source,
            dst_ref=target,
            send_sem=send,
            recv_sem=recv,
            device_id={"snap": me, "row": to},
            device_id_type=MESH,
        )

    def share_copy(r, i):
        to = (row + i) % rows
        return row_copy(
            shares.at[r, to], share_in.at[r, i], share_send.at[r, i], share_recv.at[r, i], to
        )

    def merge_copy(r):
        return row_copy(
            shares.at[r, rows - 1 - row], merge_in.at[r], merge_send.at[r], merge_recv.at[r], near
        )

    def skips(i):
        return jnp.logical_and(outer, (row + i) % rows == rows - 1 - row)

    def finish(r):
        @pl.when(outer)
        def _():
            merge_copy(r).start()

        for i in range(1, rows):

            @pl.when(jnp.logical_not(jnp.logical_or(skips(i), jnp.logical_and(inner, i == 2))))
            def _():
                share_copy(r, i).start()

    def forward(r):
        @pl.when(inner)
        def _():
            merge_copy(r).wait_recv()
            far = (row + 2) % rows
            shares[r, far] = shares[r, far] + merge_in[r]
            share_copy(r, 2).start()

    def collect(r):
        total = shares[r, row]
        gram_ref[r, 0] = total

        for i in range(1, rows):
            from_far = jnp.logical_and(outer, (row + rows - i) % rows == rows - 1 - row)

            @pl.when(jnp.logical_not(from_far))
            def _():
                share_copy(r, i).wait_recv()
                gram_ref[r, 0] += share_in[r, i]

            @pl.when(jnp.logical_not(skips(i)))
            def _():
                share_copy(r, i).wait_send()

        gram_ref[r, 0] = gram_ref[r, 0] * scale

        @pl.when(outer)
        def _():
            merge_copy(r).wait_send()

    pass_on_all()

    @pl.loop(0, GROUPS)
    def _(k):
        round_one(k)

        @pl.when(jnp.logical_and(is_helper, k == 3))
        def _():
            rot_on[0].wait_recv()
            high, low = split(rot_before[...])
            before_high[...] = high
            before_low[...] = low
            help_first(0)

        @pl.when(jnp.logical_and(is_helper, k == 5))
        def _():
            help_first(1)

        early = jnp.where(is_head, 0, 4)

        @pl.loop(jnp.where(k == 6, early, 0), jnp.where(k == 5, early, jnp.where(k == 6, 6, 0)))
        def _(j):
            round_two(j)

    @pl.when(in_high)
    def _():
        pl.semaphore_wait(rows_all_in, 1)

    finish(0)

    @pl.when(in_low)
    def _():
        forward(0)

    @pl.loop(GROUPS - 2, GROUPS)
    def _(j):
        round_two(j)

    @pl.when(in_high)
    def _():
        forward(0)

    @pl.when(row == 2)
    def _():
        forward(1)

    finish(1)

    @pl.when(row == 1)
    def _():
        forward(1)

    collect(0)
    sent = blocks.at[pl.ds(0, 2 * (run - 1) * modes)]
    pltpu.make_async_copy(sent, sent, a2a_send).wait()
    pltpu.make_async_copy(over, over, over_send).wait()

    @pl.when(jnp.logical_not(is_helper))
    def _():
        two = stage.at[pl.ds(0, 2)]
        pltpu.make_async_copy(two, two, extra_send).wait()

    @pl.when(is_helper)
    def _():
        for side in range(2):
            help_copy(side, (my_group, across_group)[side]).wait_send()

    @pl.when(is_last)
    def _():
        rot_across.wait_send()
        for copy in rot_on:
            copy.wait_send()

    @pl.when(jnp.logical_not(is_last))
    def _():
        pltpu.make_async_copy(second, second, next_send).wait()

    collect(1)


def write_results(out_from, gram_from, out_ref, gram_ref, sems):
    copies = [
        pltpu.make_async_copy(out_from, out_ref, sems.at[0]),
        pltpu.make_async_copy(gram_from, gram_ref, sems.at[1]),
    ]
    for copy in copies:
        copy.start()
    for copy in copies:
        copy.wait()


def body(delay_matrix, arrangement, rotations):
    modes, delays, columns = delay_matrix.shape
    snaps = lax.axis_size("snap")
    rows = lax.axis_size("row")
    width = columns // snaps
    half = width // 2
    share_rows = width // rows
    sizes = (snaps, rows, modes, delays, width)
    f32, bf16 = jnp.float32, jnp.bfloat16
    blocks = delay_matrix.reshape(modes, delays, 2 * snaps, half).transpose(0, 2, 1, 3)
    hbm = pl.BlockSpec(memory_space=pltpu.HBM)
    vmem = pl.BlockSpec(memory_space=pltpu.VMEM)
    out_shape = (
        jax.ShapeDtypeStruct((snaps * modes, delays, width), f32),
        jax.ShapeDtypeStruct((2, 1, share_rows, width), f32),
    )
    rotated, grams = pl.pallas_call(
        functools.partial(kernel, sizes),
        out_shape=tuple(pltpu.VMEM(s.shape, s.dtype) for s in out_shape),
        in_specs=[hbm, hbm, hbm],
        out_specs=(vmem, vmem),
        scratch_shapes=[
            pltpu.SMEM(arrangement.shape, arrangement.dtype),
            pltpu.VMEM(blocks.shape, f32),
            pltpu.VMEM(rotations.shape, f32),
            pltpu.VMEM((width, half), f32),
            pltpu.VMEM((snaps, modes, delays, width), f32),
            pltpu.VMEM((EARLY + 1, modes, delays, width), f32),
            pltpu.VMEM((EARLY + 1, modes, delays, width), f32),
            pltpu.VMEM((width, half), f32),
            pltpu.VMEM((snaps * modes, delays, width), f32),
            pltpu.VMEM((2, snaps // GROUPS * modes, delays, width), f32),
            pltpu.VMEM((2, snaps // GROUPS * modes, delays, half), f32),
            pltpu.VMEM((snaps * modes, delays, half), f32),
            pltpu.VMEM((snaps * modes, delays, half), f32),
            pltpu.VMEM((snaps * modes, delays, half), f32),
            pltpu.VMEM((2, width, width), bf16),
            pltpu.VMEM((2, width, width), bf16),
            pltpu.VMEM((width, half), bf16),
            pltpu.VMEM((width, half), bf16),
            pltpu.VMEM((2, rows, share_rows, width), f32),
            pltpu.VMEM((2, rows, share_rows, width), f32),
            pltpu.VMEM((2, share_rows, width), f32),
            pltpu.SemaphoreType.DMA((3,)),
            pltpu.SemaphoreType.DMA,
            pltpu.SemaphoreType.DMA((GROUPS,)),
            pltpu.SemaphoreType.DMA,
            pltpu.SemaphoreType.DMA((2,)),
            pltpu.SemaphoreType.DMA,
            pltpu.SemaphoreType.DMA,
            pltpu.SemaphoreType.DMA,
            pltpu.SemaphoreType.DMA((EARLY // BATCH + 1,)),
            pltpu.SemaphoreType.DMA((GROUPS // 2,)),
            pltpu.SemaphoreType.DMA,
            pltpu.SemaphoreType.DMA((2,)),
            pltpu.SemaphoreType.REGULAR,
            pltpu.SemaphoreType.REGULAR,
            pltpu.SemaphoreType.REGULAR,
            pltpu.SemaphoreType.REGULAR,
            pltpu.SemaphoreType.REGULAR,
            pltpu.SemaphoreType.DMA,
            pltpu.SemaphoreType.DMA((GROUPS,)),
            pltpu.SemaphoreType.DMA((2, rows)),
            pltpu.SemaphoreType.DMA((2, rows)),
            pltpu.SemaphoreType.DMA((2,)),
            pltpu.SemaphoreType.DMA((2,)),
        ],
        compiler_params=pltpu.CompilerParams(
            collective_id=0, has_side_effects=True, vmem_limit_bytes=60 * 1024 * 1024
        ),
        name="rounds",
    )(arrangement, blocks, rotations)
    return pl.pallas_call(
        write_results,
        out_shape=out_shape,
        in_specs=[vmem, vmem],
        out_specs=(hbm, hbm),
        scratch_shapes=[pltpu.SemaphoreType.DMA((2,))],
        name="write_results",
    )(
        pltpu.with_memory_space_constraint(rotated, pltpu.VMEM),
        pltpu.with_memory_space_constraint(grams, pltpu.VMEM),
    )


def solution(mesh):
    placed = (P("snap", "row", None), P(), P(None, "snap", None, None))
    return jax.shard_map(
        body,
        mesh=mesh,
        in_specs=placed,
        out_specs=(P(None, "row", "snap"), P(None, "snap", "row", None)),
        check_vma=False,
    )
```
